32 devices in a mesh: wide: 8 (over y, x, core), narrow: 4 (over z).
Axes of the slice: x: 2, y: 2, z: 4, core: 2. Of those that a mesh axis runs over, the one named last changes fastest.
Arguments:
- state: float32 [2, 2097152], P(None, ('wide', 'narrow')), may hold values from -6 to 6
- gates: float32 [6, 2, 256, 256], replicated
- gate_bits: int32 [6, 8], replicated, may hold values from 7 to 15, as said below
- slot_plan: int32 [5], replicated, may hold values from 7 to 15, as said below
Outputs:
- final_state: float32 [2, 2097152], P(None, ('wide', 'narrow'))
The draws below stay inside these ranges and needn't reach their ends.
Inputs may be any that keep to these rules, and one draw needn't show every extreme that they name: `gate_bits`: each gate's row names 8 different positions. `slot_plan`: the first 2 entries differ from one another, and so do the last 3.
All inputs are finite; a program needn't handle non-finite values.
Results may differ from the reference program's by a relative error of at most 0.0001.
Values sent between devices are 32-bit elements; how exact they have to be, the bound alone decides.
A program may use at most 64 MiB of HBM per device.

```python
import jax
import jax.numpy as jnp
from jax import lax

GATE_QUBITS = 8
GATE_DIM = 256
GATES = 6
LANE_BITS = 7
LOCAL = 16
NARROW_BITS = 2
WIDE_BITS = 3
TOTAL = 2097152


def draw_gates(key, part):
    keys = jax.random.split(jax.random.fold_in(key, 11), 2)
    real_part = jax.random.normal(keys[0], (GATES, GATE_DIM, GATE_DIM), jnp.float32)
    imag_part = jax.random.normal(keys[1], (GATES, GATE_DIM, GATE_DIM), jnp.float32)
    matrix = lax.complex(real_part, imag_part)
    unitary_q, upper = jnp.linalg.qr(matrix)
    diagonal = jnp.diagonal(upper, axis1=-2, axis2=-1)
    phases = diagonal / jnp.abs(diagonal)
    unitary = unitary_q * phases[:, None, :]
    return jnp.stack([jnp.real(unitary), jnp.imag(unitary)], axis=1).astype(jnp.float32)


def draw_gate_bits(key, part):
    base = jax.random.fold_in(key, 23)
    rows = []
    for index in range(GATES):
        chosen = jax.random.permutation(jax.random.fold_in(base, index), LOCAL - LANE_BITS)[:GATE_QUBITS]
        rows.append((chosen + LANE_BITS).astype(jnp.int32))
    return jnp.stack(rows).astype(jnp.int32)


def draw_slot_plan(key, part):
    base = jax.random.fold_in(key, 37)
    first = jax.random.permutation(jax.random.fold_in(base, 1), LOCAL - LANE_BITS)[:NARROW_BITS]
    second = jax.random.permutation(jax.random.fold_in(base, 2), LOCAL - LANE_BITS)[:WIDE_BITS]
    return (jnp.concatenate([first, second]) + LANE_BITS).astype(jnp.int32)


def block_scale(stream_key, shape, shards, least, top_value):
    gain = 1.0
    for position, blocks in shards:
        draws = jax.random.uniform(jax.random.fold_in(jax.random.fold_in(stream_key, 6), position), (blocks,), jnp.float32, least / len(shards), top_value / len(shards))
        gain = gain * jnp.repeat(jnp.exp(draws), shape[position] // blocks).reshape((-1,) + (1,) * (len(shape) - 1 - position))
    return gain


def scatter_about(key, extent, width, bound, shards=(), kind=jnp.bfloat16):
    values = width * jax.random.normal(key, extent, jnp.float32)
    if shards:
        values = values * block_scale(key, extent, shards, -0.22, 0.18)
    return jnp.clip(values, -bound, bound).astype(kind)


def setup_inputs(seed: int = 0) -> dict:
    splits = jax.random.split(jax.random.key(seed), 5)
    state = scatter_about(splits[0], (2, TOTAL), 1.0, 6.0, ((1, 32),), jnp.float32)
    gates = draw_gates(jax.random.fold_in(splits[4], 71), 0)
    gate_bits = draw_gate_bits(jax.random.fold_in(splits[4], 71), 0)
    slot_plan = draw_slot_plan(jax.random.fold_in(splits[4], 71), 0)
    return dict(state=state, gates=gates, gate_bits=gate_bits, slot_plan=slot_plan)


def bit_table(weights, nbits):
    low_count = nbits // 2
    high_count = nbits - low_count

    def partial_table(count, offset):
        values = jnp.arange(2 ** count, dtype=jnp.int32)
        places = jnp.arange(count, dtype=jnp.int32)
        bits_of = values[:, None] >> places[None, :] & 1
        return jnp.sum(bits_of * weights[offset:offset + count][None, :], axis=1).astype(jnp.int32)
    return (partial_table(high_count, low_count)[:, None] + partial_table(low_count, 0)[None, :]).reshape(-1).astype(jnp.int32)

def gate_order(qubits, nbits):
    count = qubits.shape[0]
    positions = jnp.arange(nbits, dtype=jnp.int32)
    hits = (positions[:, None] == qubits[None, :]).astype(jnp.int32)
    free_flag = (1 - jnp.sum(hits, axis=1)).astype(jnp.int32)
    ranks = (jnp.cumsum(free_flag) - free_flag).astype(jnp.int32)
    targets = jnp.arange(nbits - count, dtype=jnp.int32)
    picked = (ranks[None, :] == targets[:, None]) & (free_flag[None, :] == 1)
    others = jnp.sum(picked.astype(jnp.int32) * positions[None, :], axis=1).astype(jnp.int32)
    return jnp.concatenate([others, qubits.astype(jnp.int32)]).astype(jnp.int32)

def inverse_weights(order, nbits):
    positions = jnp.arange(nbits, dtype=jnp.int32)
    powers = jnp.left_shift(jnp.int32(1), positions)
    match = (order[None, :] == positions[:, None]).astype(jnp.int32)
    return jnp.sum(match * powers[None, :], axis=1).astype(jnp.int32)

def apply_gate(state, unitary, qubits, nbits):
    order = gate_order(qubits, nbits)
    forward = bit_table(jnp.left_shift(jnp.int32(1), order), nbits)
    moved = state[:, forward]
    dim = unitary.shape[-1]
    moved = moved.reshape(2, dim, -1)
    high = lax.Precision.HIGHEST
    real_part = jnp.dot(unitary[0].astype(jnp.float32), moved[0].astype(jnp.float32), precision=high, preferred_element_type=jnp.float32) - jnp.dot(unitary[1].astype(jnp.float32), moved[1].astype(jnp.float32), precision=high, preferred_element_type=jnp.float32)
    imag_part = jnp.dot(unitary[0].astype(jnp.float32), moved[1].astype(jnp.float32), precision=high, preferred_element_type=jnp.float32) + jnp.dot(unitary[1].astype(jnp.float32), moved[0].astype(jnp.float32), precision=high, preferred_element_type=jnp.float32)
    result = jnp.stack([real_part, imag_part]).reshape(2, -1)
    return result[:, bit_table(inverse_weights(order, nbits), nbits)]

def swap_state(state, nbits, firsts, seconds):
    positions = jnp.arange(nbits, dtype=jnp.int32)
    weights = jnp.left_shift(jnp.int32(1), positions)
    for number in range(len(firsts)):
        upper = jnp.int32(firsts[number])
        lower = seconds[number].astype(jnp.int32)
        weights = jnp.where(positions == upper, jnp.left_shift(jnp.int32(1), lower), jnp.where(positions == lower, jnp.left_shift(jnp.int32(1), upper), weights)).astype(jnp.int32)
    return state[:, bit_table(weights, nbits)]

def reference(state, gates, gate_bits, slot_plan):
    nbits = LOCAL + NARROW_BITS + WIDE_BITS
    third = GATES // 3
    for index in range(third):
        state = apply_gate(state, gates[index], gate_bits[index], nbits)
    state = swap_state(state, nbits, [LOCAL + b for b in range(NARROW_BITS)], [slot_plan[b] for b in range(NARROW_BITS)])
    for index in range(third, 2 * third):
        state = apply_gate(state, gates[index], gate_bits[index], nbits)
    state = swap_state(state, nbits, [LOCAL + NARROW_BITS + b for b in range(WIDE_BITS)], [slot_plan[NARROW_BITS + b] for b in range(WIDE_BITS)])
    for index in range(2 * third, GATES):
        state = apply_gate(state, gates[index], gate_bits[index], nbits)
    return state
```

```python
import functools

import jax
import jax.numpy as jnp
from jax import lax
from jax.experimental import pallas as pl
from jax.experimental.pallas import tpu as pltpu
from jax.sharding import PartitionSpec as P

LANE_BITS = 7
LANES = 2**LANE_BITS
HALF = LANES // 2
CHUNKS = 2
MESH = pl.DeviceIdType.MESH
F32 = jnp.float32
BF16 = jnp.bfloat16


def log2(value):
    return value.bit_length() - 1


def one_hot(lane_values, rows):
    columns = lane_values.shape[1]
    row = lax.broadcasted_iota(jnp.int32, (rows, columns), 0)
    return jnp.where(row == lane_values, 1.0, 0.0).astype(BF16)


def split(values):
    high = values.astype(BF16)
    return high, (values - high.astype(F32)).astype(BF16)


def dot(a, b):
    return jnp.dot(a, b, preferred_element_type=F32)


class Layout:
    def __init__(self, free, wanted, row_bits):
        self.free = free
        self.row_bits = row_bits
        seen = jnp.int32(1) << free
        left = jnp.int32(row_bits - 2)
        packed = jnp.int32(0)
        for label in wanted:
            new = 1 - ((seen >> label) & 1)
            packed = packed + ((new * left) << (3 * label))
            left = left - new
            seen = seen | (jnp.int32(1) << label)
        for label in range(row_bits):
            new = 1 - ((seen >> label) & 1)
            packed = packed + ((new * left) << (3 * label))
            left = left - new
        self.packed = packed

    def inner(self, label):
        return (self.packed >> (3 * label)) & 7

    def shift(self, label):
        return jnp.where(label == self.free, self.row_bits - 1, self.inner(label))


def local_move(layout, free_next):
    differs = layout.free != free_next
    weights = [jnp.where(differs, 2, 1), jnp.where(differs, 1, 2)]

    def place(label):
        return jnp.where(label == layout.free, layout.row_bits - 2, layout.inner(label))

    return weights, place


def exchange_move(layout, slots, free_next):
    top = len(slots) + 2
    base = layout.row_bits - top
    slot_places = [layout.shift(slot) - base for slot in slots]
    count = jnp.int32(0)
    low = [jnp.int32(0), jnp.int32(0)]
    sent_places = []
    for index in range(top):
        is_slot = jnp.int32(0)
        value = jnp.int32(0)
        for number, slot_place in enumerate(slot_places):
            hit = (slot_place == index).astype(jnp.int32)
            is_slot = is_slot + hit
            value = value + hit * (2 + number)
        sent_places.append(jnp.where(is_slot == 1, value, count))
        for number in range(2):
            low[number] = low[number] + jnp.where(
                (is_slot == 0) & (count == number), 1 << index, 0
            )
        count = count + 1 - is_slot
    send_weights = low + [jnp.int32(1) << slot_place for slot_place in slot_places]

    def look_up(table, position):
        total = jnp.int32(0)
        for index, entry in enumerate(table):
            total = total + jnp.where(position == index, entry, 0)
        return total

    free_place = look_up(sent_places, layout.shift(free_next) - base)
    load_weights = [
        jnp.where(free_place <= index, 2 << index, 1 << index) for index in range(top - 1)
    ] + [jnp.int32(1) << free_place]
    final = [
        place - jnp.where(place > free_place, 1, 0) for place in sent_places
    ]

    def place(label):
        shift = layout.shift(label)
        return jnp.where(shift < base, shift, base + look_up(final, shift - base))

    return send_weights, load_weights, place


def block_number(index, weights):
    total = jnp.int32(0)
    for bit, weight in enumerate(weights):
        if (index >> bit) & 1:
            total = total + weight
    return total & (2 ** len(weights) - 1)


def load_blocks(ref, weights):
    count, rows, _ = ref.shape
    halves = []
    for half in range(2):
        parts = [
            ref[block_number(half * (count // 2) + index, weights)]
            for index in range(count // 2)
        ]
        halves.append(jnp.concatenate(parts, axis=0))
    return jnp.concatenate(halves, axis=1)


def store_blocks(ref, halves):
    count, rows, lanes = ref.shape
    for half in range(2):
        ref[pl.ds(half * (count // 2), count // 2)] = halves[half].reshape(
            count // 2, rows, lanes
        )


def kernel(
    narrow,
    wide,
    bits_ref,
    plan_ref,
    state_hbm,
    gates_hbm,
    out_ref,
    state_ref,
    gates_ref,
    high_ref,
    low_ref,
    local_ref,
    narrow_out,
    narrow_send,
    narrow_recv_0,
    narrow_recv_1,
    wide_out,
    wide_send,
    wide_recv_0,
    wide_recv_1,
    state_sem,
    gate_sem,
    narrow_send_sem,
    narrow_recv_sem,
    wide_send_sem,
    wide_recv_sem,
):
    gate_count, _, dim, _ = gates_ref.shape
    third = gate_count // 3
    qubits = log2(dim)
    rows = state_ref.shape[0] // 2
    row_bits = log2(rows)
    narrow_bits = log2(narrow)
    wide_bits = log2(wide)
    me = {"narrow": lax.axis_index("narrow"), "wide": lax.axis_index("wide")}
    sizes = {"narrow": narrow, "wide": wide}
    narrow_recv = (narrow_recv_0, narrow_recv_1)
    wide_recv = (wide_recv_0, wide_recv_1)

    state_copy = pltpu.make_async_copy(state_hbm, state_ref, state_sem)
    state_copy.start()
    gate_copies = []
    for k in range(gate_count):
        gate_copies.append(
            pltpu.make_async_copy(gates_hbm.at[k], gates_ref.at[k], gate_sem.at[k])
        )
        gate_copies[-1].start()

    barrier = pltpu.get_barrier_semaphore()
    for axis in ("narrow", "wide"):
        for step in range(1, sizes[axis]):
            peer = lax.rem(me[axis] + step, sizes[axis])
            pl.semaphore_signal(
                barrier, inc=1, device_id={axis: peer}, device_id_type=MESH
            )

    targets = [
        [bits_ref[k * qubits + j] - LANE_BITS for j in range(qubits)]
        for k in range(gate_count)
    ]
    free = [sum(range(row_bits)) - sum(targets[k]) for k in range(gate_count)]
    slots = [plan_ref[b] - LANE_BITS for b in range(narrow_bits + wide_bits)]
    crossing = {
        third - 1: slots[:narrow_bits],
        2 * third - 1: slots[narrow_bits:],
    }
    layouts, loads, sends, places = {}, {}, {}, {}

    def plan(k):
        layouts[k] = Layout(free[k], crossing.get(k, []) + [free[k + 1]], row_bits)
        if k in crossing:
            sends[k], loads[k], places[k + 1] = exchange_move(
                layouts[k], crossing[k], free[k + 1]
            )
        else:
            loads[k], places[k + 1] = local_move(layouts[k], free[k + 1])

    lane = lax.broadcasted_iota(jnp.int32, (1, dim), 1)

    def prepare(k):
        gate_copies[k].wait()
        pieces = [split(gates_ref[k, part]) for part in range(2)]
        if k > 0:
            column = sum(((lane >> places[k](targets[k][j])) & 1) << j for j in range(qubits))
            pick = one_hot(column, dim)
            pieces = [
                [dot(piece, pick).astype(BF16) for piece in both] for both in pieces
            ]
        if k < gate_count - 1:
            row = sum(
                ((lane >> j) & 1) << layouts[k].inner(targets[k][j]) for j in range(qubits)
            )
            pick_row = one_hot(row, dim)
            pieces = [
                [dot(pick_row, piece).astype(BF16) for piece in both] for both in pieces
            ]
        for part in range(2):
            high_ref[k, pl.ds(part * dim, dim)] = pieces[part][0]
            low_ref[k, pl.ds(part * dim, dim)] = pieces[part][1]

    first_half = lax.broadcasted_iota(jnp.int32, (dim, LANES), 1) < HALF

    def apply(k, halves):
        high, low = split(halves)
        total = dot(high_ref[k], high) + dot(high_ref[k], low) + dot(low_ref[k], high)
        results = []
        for half in range(2):
            by_real = total[:dim, half * LANES : (half + 1) * LANES]
            by_imag = pltpu.roll(
                total[dim:, half * LANES : (half + 1) * LANES], HALF, 1
            )
            results.append(by_real + jnp.where(first_half, -by_imag, by_imag))
        return results

    def copy_to(axis, chunk, send_ref, recv_ref, send_sems, recv_sems, peer):
        start = pl.ds(peer * 4, 4)
        return pltpu.make_async_remote_copy(
            src_ref=send_ref.at[chunk, start],
            dst_ref=recv_ref[chunk].at[pl.ds(me[axis] * 4, 4)],
            send_sem=send_sems.at[chunk, peer],
            recv_sem=recv_sems.at[chunk, me[axis]],
            device_id={axis: peer},
            device_id_type=MESH,
        )

    def copy_from(axis, chunk, send_ref, recv_ref, send_sems, recv_sems, peer):
        start = pl.ds(peer * 4, 4)
        return pltpu.make_async_remote_copy(
            src_ref=send_ref.at[chunk, start],
            dst_ref=recv_ref[chunk].at[start],
            send_sem=send_sems.at[chunk, peer],
            recv_sem=recv_sems.at[chunk, peer],
            device_id={axis: peer},
            device_id_type=MESH,
        )

    links = {
        "narrow": (narrow_send, narrow_recv, narrow_send_sem, narrow_recv_sem),
        "wide": (wide_send, wide_recv, wide_send_sem, wide_recv_sem),
    }

    def send(k, axis, chunk, out):
        send_ref, recv_ref = links[axis][:2]
        for index in range(out.shape[0]):
            send_ref[chunk, index] = out[block_number(index, sends[k])]
        for step in range(1, sizes[axis]):
            peer = lax.rem(me[axis] + step, sizes[axis])
            copy_to(axis, chunk, *links[axis], peer).start()
        own = pl.ds(me[axis] * 4, 4)
        recv_ref[chunk][own] = send_ref[chunk, own]

    def receive(axis, chunk):
        for step in range(1, sizes[axis]):
            peer = lax.rem(me[axis] + sizes[axis] - step, sizes[axis])
            copy_from(axis, chunk, *links[axis], peer).wait_recv()

    def section(first, chunk, halves, out):
        for k in range(first, first + third):
            results = apply(k, halves)
            if k < first + third - 1:
                held = local_ref.at[first // third, chunk]
                store_blocks(held, results)
                halves = load_blocks(held, loads[k])
        if out is not None:
            store_blocks(out, results)
        return results

    for k in range(third):
        plan(k)
    source = lax.broadcasted_iota(jnp.int32, (1, rows), 1)
    target = ((source >> free[0]) & 1) << (row_bits - 1)
    for j in range(qubits):
        target = target + (((source >> targets[0][j]) & 1) << j)
    order_in = one_hot(target, rows)
    prepare(0)
    state_copy.wait()
    real, imag = (state_ref[pl.ds(part, rows, stride=2), :] for part in range(2))
    whole_half = lax.broadcasted_iota(jnp.int32, (rows, LANES), 1) < HALF
    packed = [
        jnp.where(whole_half, real, pltpu.roll(imag, HALF, 1)),
        jnp.where(whole_half, pltpu.roll(real, HALF, 1), imag),
    ]
    for k in range(1, third):
        prepare(k)
    for chunk in range(CHUNKS):
        high, low = split(packed[chunk])
        ordered = dot(order_in, high) + dot(order_in, low)
        halves = jnp.concatenate([ordered[:dim], ordered[dim:]], axis=1)
        out = narrow_out.at[chunk]
        section(0, chunk, halves, out)
        if chunk == 0:
            pl.semaphore_wait(barrier, narrow + wide - 2)
        send(third - 1, "narrow", chunk, out)

    for k in range(third, gate_count - 1):
        plan(k)
    for k in range(third, gate_count):
        prepare(k)
    source = lax.broadcasted_iota(jnp.int32, (1, rows), 1)
    target = ((source >> (row_bits - 1)) & 1) << free[gate_count - 1]
    for j in range(qubits):
        target = target + (((source >> j) & 1) << targets[gate_count - 1][j])
    order_out = one_hot(target, rows)

    for chunk in range(CHUNKS):
        receive("narrow", chunk)
        halves = load_blocks(narrow_recv[chunk], loads[third - 1])
        out = wide_out.at[chunk]
        section(third, chunk, halves, out)
        send(2 * third - 1, "wide", chunk, out)

    final = []
    for chunk in range(CHUNKS):
        receive("wide", chunk)
        halves = load_blocks(wide_recv[chunk], loads[2 * third - 1])
        results = section(2 * third, chunk, halves, None)
        high, low = split(jnp.concatenate(results, axis=0))
        final.append(dot(order_out, high) + dot(order_out, low))
    out_ref[pl.ds(0, rows, stride=2), :] = jnp.where(
        whole_half, final[0], pltpu.roll(final[1], HALF, 1)
    )
    out_ref[pl.ds(1, rows, stride=2), :] = jnp.where(
        whole_half, pltpu.roll(final[0], HALF, 1), final[1]
    )

    for axis in ("narrow", "wide"):
        for chunk in range(CHUNKS):
            for step in range(1, sizes[axis]):
                peer = lax.rem(me[axis] + step, sizes[axis])
                copy_to(axis, chunk, *links[axis], peer).wait_send()


def shards(state, gates, gate_bits, slot_plan):
    amount = state.shape[1]
    rows = amount // LANES
    narrow = lax.axis_size("narrow")
    wide = lax.axis_size("wide")
    gate_count, _, dim, _ = gates.shape

    def exchange_buffers(size):
        count = 4 * size
        block = (count, rows // count, LANES)
        return [pltpu.VMEM((CHUNKS, *block), F32)] * 2 + [pltpu.VMEM(block, F32)] * CHUNKS

    def sems(size):
        return [pltpu.SemaphoreType.DMA((CHUNKS, size))] * 2

    mixed = state.reshape(2, rows, LANES).transpose(1, 0, 2).reshape(2 * rows, LANES)
    result = pl.pallas_call(
        functools.partial(kernel, narrow, wide),
        out_shape=jax.ShapeDtypeStruct((2 * rows, LANES), F32),
        in_specs=[
            pl.BlockSpec(memory_space=pltpu.SMEM),
            pl.BlockSpec(memory_space=pltpu.SMEM),
            pl.BlockSpec(memory_space=pl.ANY),
            pl.BlockSpec(memory_space=pl.ANY),
        ],
        out_specs=pl.BlockSpec(memory_space=pltpu.VMEM),
        scratch_shapes=[
            pltpu.VMEM((2 * rows, LANES), F32),
            pltpu.VMEM(gates.shape, F32),
            pltpu.VMEM((gate_count, 2 * dim, dim), BF16),
            pltpu.VMEM((gate_count, 2 * dim, dim), BF16),
            pltpu.VMEM((3, CHUNKS, 4, rows // 4, LANES), F32),
            *exchange_buffers(narrow),
            *exchange_buffers(wide),
            pltpu.SemaphoreType.DMA,
            pltpu.SemaphoreType.DMA((gate_count,)),
            *sems(narrow),
            *sems(wide),
        ],
        compiler_params=pltpu.CompilerParams(
            collective_id=0, has_side_effects=True, vmem_limit_bytes=48 * 2**20
        ),
        name="window",
    )(gate_bits.reshape(-1), slot_plan, mixed, gates)
    return result.reshape(rows, 2, LANES).transpose(1, 0, 2).reshape(2, amount)


def solution(mesh):
    return jax.shard_map(
        shards,
        mesh=mesh,
        in_specs=(P(None, ("wide", "narrow")), P(), P(), P()),
        out_specs=P(None, ("wide", "narrow")),
        check_vma=False,
    )
```

```python
import functools

import jax
import jax.numpy as jnp
from jax import lax
from jax.experimental import pallas as pl
from jax.experimental.pallas import tpu as pltpu
from jax.sharding import PartitionSpec as P

LANE_BITS = 7
LANES = 2**LANE_BITS
HALF = LANES // 2
CHUNKS = 2
MESH = pl.DeviceIdType.MESH
F32 = jnp.float32
BF16 = jnp.bfloat16


def log2(value):
    return value.bit_length() - 1


def partner(index, distance):
    result = index
    bit = 1
    while bit <= distance:
        if distance & bit:
            result = result + bit - 2 * bit * lax.rem(lax.div(index, bit), 2)
        bit *= 2
    return result


def one_hot(lane_values, rows):
    columns = lane_values.shape[1]
    row = lax.broadcasted_iota(jnp.int32, (rows, columns), 0)
    return jnp.where(row == lane_values, 1.0, 0.0).astype(BF16)


def split(values):
    high = values.astype(BF16)
    return high, (values - high.astype(F32)).astype(BF16)


def dot(a, b):
    return jnp.dot(a, b, preferred_element_type=F32)


class Layout:
    def __init__(self, free, wanted, row_bits):
        self.free = free
        self.row_bits = row_bits
        seen = jnp.int32(1) << free
        left = jnp.int32(row_bits - 2)
        packed = jnp.int32(0)
        for label in wanted:
            new = 1 - ((seen >> label) & 1)
            packed = packed + ((new * left) << (3 * label))
            left = left - new
            seen = seen | (jnp.int32(1) << label)
        for label in range(row_bits):
            new = 1 - ((seen >> label) & 1)
            packed = packed + ((new * left) << (3 * label))
            left = left - new
        self.packed = packed

    def inner(self, label):
        return (self.packed >> (3 * label)) & 7

    def shift(self, label):
        return jnp.where(label == self.free, self.row_bits - 1, self.inner(label))


def local_move(layout, free_next):
    differs = layout.free != free_next
    weights = [jnp.where(differs, 2, 1), jnp.where(differs, 1, 2)]

    def place(label):
        return jnp.where(label == layout.free, layout.row_bits - 2, layout.inner(label))

    return weights, place


def exchange_move(layout, slots, free_next):
    top = len(slots) + 2
    base = layout.row_bits - top
    slot_places = [layout.shift(slot) - base for slot in slots]
    count = jnp.int32(0)
    low = [jnp.int32(0), jnp.int32(0)]
    sent_places = []
    for index in range(top):
        is_slot = jnp.int32(0)
        value = jnp.int32(0)
        for number, slot_place in enumerate(slot_places):
            hit = (slot_place == index).astype(jnp.int32)
            is_slot = is_slot + hit
            value = value + hit * (2 + number)
        sent_places.append(jnp.where(is_slot == 1, value, count))
        for number in range(2):
            low[number] = low[number] + jnp.where(
                (is_slot == 0) & (count == number), 1 << index, 0
            )
        count = count + 1 - is_slot
    send_weights = low + [jnp.int32(1) << slot_place for slot_place in slot_places]

    def look_up(table, position):
        total = jnp.int32(0)
        for index, entry in enumerate(table):
            total = total + jnp.where(position == index, entry, 0)
        return total

    free_place = look_up(sent_places, layout.shift(free_next) - base)
    load_weights = [
        jnp.where(free_place <= index, 2 << index, 1 << index) for index in range(top - 1)
    ] + [jnp.int32(1) << free_place]
    final = [
        place - jnp.where(place > free_place, 1, 0) for place in sent_places
    ]

    def place(label):
        shift = layout.shift(label)
        return jnp.where(shift < base, shift, base + look_up(final, shift - base))

    return send_weights, load_weights, place


def block_number(index, weights):
    total = jnp.int32(0)
    for bit, weight in enumerate(weights):
        if (index >> bit) & 1:
            total = total + weight
    return total & (2 ** len(weights) - 1)


def load_blocks(ref, weights):
    count, rows, _ = ref.shape
    halves = []
    for half in range(2):
        parts = [
            ref[block_number(half * (count // 2) + index, weights)]
            for index in range(count // 2)
        ]
        halves.append(jnp.concatenate(parts, axis=0))
    return jnp.concatenate(halves, axis=1)


def store_blocks(ref, halves):
    count, rows, lanes = ref.shape
    for half in range(2):
        ref[pl.ds(half * (count // 2), count // 2)] = halves[half].reshape(
            count // 2, rows, lanes
        )


def kernel(
    narrow,
    wide,
    bits_ref,
    plan_ref,
    state_hbm,
    gates_hbm,
    out_ref,
    state_ref,
    gates_ref,
    high_ref,
    low_ref,
    local_ref,
    narrow_out,
    narrow_send,
    narrow_recv_0,
    narrow_recv_1,
    wide_out,
    wide_send,
    wide_recv_0,
    wide_recv_1,
    state_sem,
    gate_sem,
    narrow_send_sem,
    narrow_recv_sem,
    wide_send_sem,
    wide_recv_sem,
):
    gate_count, _, dim, _ = gates_ref.shape
    third = gate_count // 3
    qubits = log2(dim)
    rows = state_ref.shape[0] // 2
    row_bits = log2(rows)
    narrow_bits = log2(narrow)
    wide_bits = log2(wide)
    me = {"narrow": lax.axis_index("narrow"), "wide": lax.axis_index("wide")}
    sizes = {"narrow": narrow, "wide": wide}
    narrow_recv = (narrow_recv_0, narrow_recv_1)
    wide_recv = (wide_recv_0, wide_recv_1)

    state_copy = pltpu.make_async_copy(state_hbm, state_ref, state_sem)
    state_copy.start()
    gate_copies = []
    for k in range(gate_count):
        gate_copies.append(
            pltpu.make_async_copy(gates_hbm.at[k], gates_ref.at[k], gate_sem.at[k])
        )
        gate_copies[-1].start()

    barrier = pltpu.get_barrier_semaphore()
    for axis in ("narrow", "wide"):
        for step in reversed(range(1, sizes[axis])):
            peer = partner(me[axis], step)
            pl.semaphore_signal(
                barrier, inc=1, device_id={axis: peer}, device_id_type=MESH
            )

    targets = [
        [bits_ref[k, j] - LANE_BITS for j in range(qubits)]
        for k in range(gate_count)
    ]
    free = [sum(range(row_bits)) - sum(targets[k]) for k in range(gate_count)]
    slots = [plan_ref[b] - LANE_BITS for b in range(narrow_bits + wide_bits)]
    crossing = {
        third - 1: slots[:narrow_bits],
        2 * third - 1: slots[narrow_bits:],
    }
    layouts, loads, sends, places = {}, {}, {}, {}

    def plan(k):
        layouts[k] = Layout(free[k], crossing.get(k, []) + [free[k + 1]], row_bits)
        if k in crossing:
            sends[k], loads[k], places[k + 1] = exchange_move(
                layouts[k], crossing[k], free[k + 1]
            )
        else:
            loads[k], places[k + 1] = local_move(layouts[k], free[k + 1])

    lane = lax.broadcasted_iota(jnp.int32, (1, dim), 1)

    def prepare(k):
        gate_copies[k].wait()
        pieces = [split(gates_ref[k, part]) for part in range(2)]
        if k > 0:
            column = sum(((lane >> places[k](targets[k][j])) & 1) << j for j in range(qubits))
            pick = one_hot(column, dim)
            pieces = [
                [dot(piece, pick).astype(BF16) for piece in both] for both in pieces
            ]
        if k < gate_count - 1:
            row = sum(
                ((lane >> j) & 1) << layouts[k].inner(targets[k][j]) for j in range(qubits)
            )
            pick_row = one_hot(row, dim)
            pieces = [
                [dot(pick_row, piece).astype(BF16) for piece in both] for both in pieces
            ]
        for part in range(2):
            high_ref[k, pl.ds(part * dim, dim)] = pieces[part][0]
            low_ref[k, pl.ds(part * dim, dim)] = pieces[part][1]

    first_half = lax.broadcasted_iota(jnp.int32, (dim, LANES), 1) < HALF

    def apply(k, halves):
        high, low = split(halves)
        total = dot(high_ref[k], high) + dot(high_ref[k], low) + dot(low_ref[k], high)
        results = []
        for half in range(2):
            by_real = total[:dim, half * LANES : (half + 1) * LANES]
            by_imag = pltpu.roll(
                total[dim:, half * LANES : (half + 1) * LANES], HALF, 1
            )
            results.append(by_real + jnp.where(first_half, -by_imag, by_imag))
        return results

    def copy_to(axis, chunk, send_ref, recv_ref, send_sems, recv_sems, peer):
        start = pl.ds(peer * 4, 4)
        return pltpu.make_async_remote_copy(
            src_ref=send_ref.at[chunk, start],
            dst_ref=recv_ref[chunk].at[pl.ds(me[axis] * 4, 4)],
            send_sem=send_sems.at[chunk, peer],
            recv_sem=recv_sems.at[chunk, me[axis]],
            device_id={axis: peer},
            device_id_type=MESH,
        )

    def copy_from(axis, chunk, send_ref, recv_ref, send_sems, recv_sems, peer):
        start = pl.ds(peer * 4, 4)
        return pltpu.make_async_remote_copy(
            src_ref=send_ref.at[chunk, start],
            dst_ref=recv_ref[chunk].at[start],
            send_sem=send_sems.at[chunk, peer],
            recv_sem=recv_sems.at[chunk, peer],
            device_id={axis: peer},
            device_id_type=MESH,
        )

    links = {
        "narrow": (narrow_send, narrow_recv, narrow_send_sem, narrow_recv_sem),
        "wide": (wide_send, wide_recv, wide_send_sem, wide_recv_sem),
    }

    def send(k, axis, chunk, out):
        send_ref, recv_ref = links[axis][:2]
        for index in range(out.shape[0]):
            send_ref[chunk, index] = out[block_number(index, sends[k])]
        for step in reversed(range(1, sizes[axis])):
            peer = partner(me[axis], step)
            copy_to(axis, chunk, *links[axis], peer).start()
        own = pl.ds(me[axis] * 4, 4)
        recv_ref[chunk][own] = send_ref[chunk, own]

    def receive(axis, chunk):
        for step in reversed(range(1, sizes[axis])):
            peer = partner(me[axis], step)
            copy_from(axis, chunk, *links[axis], peer).wait_recv()

    def section(first, chunk, halves, out):
        for k in range(first, first + third):
            results = apply(k, halves)
            if k < first + third - 1:
                held = local_ref.at[first // third, chunk]
                store_blocks(held, results)
                halves = load_blocks(held, loads[k])
        if out is not None:
            store_blocks(out, results)
        return results

    for k in range(third):
        plan(k)
    source = lax.broadcasted_iota(jnp.int32, (1, rows), 1)
    target = ((source >> free[0]) & 1) << (row_bits - 1)
    for j in range(qubits):
        target = target + (((source >> targets[0][j]) & 1) << j)
    order_in = one_hot(target, rows)
    prepare(0)
    state_copy.wait()
    real, imag = (state_ref[pl.ds(part, rows, stride=2), :] for part in range(2))
    whole_half = lax.broadcasted_iota(jnp.int32, (rows, LANES), 1) < HALF
    packed = [
        jnp.where(whole_half, real, pltpu.roll(imag, HALF, 1)),
        jnp.where(whole_half, pltpu.roll(real, HALF, 1), imag),
    ]
    for k in range(1, third):
        prepare(k)
    for chunk in range(CHUNKS):
        high, low = split(packed[chunk])
        ordered = dot(order_in, high) + dot(order_in, low)
        halves = jnp.concatenate([ordered[:dim], ordered[dim:]], axis=1)
        out = narrow_out.at[chunk]
        section(0, chunk, halves, out)
        if chunk == 0:
            pl.semaphore_wait(barrier, narrow + wide - 2)
        send(third - 1, "narrow", chunk, out)

    for k in range(third, gate_count - 1):
        plan(k)
    for k in range(third, gate_count):
        prepare(k)
    source = lax.broadcasted_iota(jnp.int32, (1, rows), 1)
    target = ((source >> (row_bits - 1)) & 1) << free[gate_count - 1]
    for j in range(qubits):
        target = target + (((source >> j) & 1) << targets[gate_count - 1][j])
    order_out = one_hot(target, rows)

    for chunk in range(CHUNKS):
        receive("narrow", chunk)
        halves = load_blocks(narrow_recv[chunk], loads[third - 1])
        out = wide_out.at[chunk]
        section(third, chunk, halves, out)
        send(2 * third - 1, "wide", chunk, out)

    final = []
    for chunk in range(CHUNKS):
        receive("wide", chunk)
        halves = load_blocks(wide_recv[chunk], loads[2 * third - 1])
        results = section(2 * third, chunk, halves, None)
        high, low = split(jnp.concatenate(results, axis=0))
        final.append(dot(order_out, high) + dot(order_out, low))
    out_ref[pl.ds(0, rows, stride=2), :] = jnp.where(
        whole_half, final[0], pltpu.roll(final[1], HALF, 1)
    )
    out_ref[pl.ds(1, rows, stride=2), :] = jnp.where(
        whole_half, pltpu.roll(final[0], HALF, 1), final[1]
    )

    for axis in ("narrow", "wide"):
        for chunk in range(CHUNKS):
            for step in reversed(range(1, sizes[axis])):
                peer = partner(me[axis], step)
                copy_to(axis, chunk, *links[axis], peer).wait_send()


def shards(state, gates, gate_bits, slot_plan):
    amount = state.shape[1]
    rows = amount // LANES
    narrow = lax.axis_size("narrow")
    wide = lax.axis_size("wide")
    gate_count, _, dim, _ = gates.shape

    def exchange_buffers(size):
        count = 4 * size
        block = (count, rows // count, LANES)
        return [pltpu.VMEM((CHUNKS, *block), F32)] * 2 + [pltpu.VMEM(block, F32)] * CHUNKS

    def sems(size):
        return [pltpu.SemaphoreType.DMA((CHUNKS, size))] * 2

    mixed = state.reshape(2, rows, LANES).transpose(1, 0, 2).reshape(2 * rows, LANES)
    result = pl.pallas_call(
        functools.partial(kernel, narrow, wide),
        out_shape=jax.ShapeDtypeStruct((2 * rows, LANES), F32),
        in_specs=[
            pl.BlockSpec(memory_space=pltpu.SMEM),
            pl.BlockSpec(memory_space=pltpu.SMEM),
            pl.BlockSpec(memory_space=pltpu.HBM),
            pl.BlockSpec(memory_space=pltpu.HBM),
        ],
        out_specs=pl.BlockSpec(memory_space=pltpu.VMEM),
        scratch_shapes=[
            pltpu.VMEM((2 * rows, LANES), F32),
            pltpu.VMEM(gates.shape, F32),
            pltpu.VMEM((gate_count, 2 * dim, dim), BF16),
            pltpu.VMEM((gate_count, 2 * dim, dim), BF16),
            pltpu.VMEM((3, CHUNKS, 4, rows // 4, LANES), F32),
            *exchange_buffers(narrow),
            *exchange_buffers(wide),
            pltpu.SemaphoreType.DMA,
            pltpu.SemaphoreType.DMA((gate_count,)),
            *sems(narrow),
            *sems(wide),
        ],
        compiler_params=pltpu.CompilerParams(
            collective_id=0, has_side_effects=True, vmem_limit_bytes=60 * 2**20
        ),
        name="window",
    )(gate_bits, slot_plan, mixed, gates)
    return result.reshape(rows, 2, LANES).transpose(1, 0, 2).reshape(2, amount)


def solution(mesh):
    return jax.shard_map(
        shards,
        mesh=mesh,
        in_specs=(P(None, ("wide", "narrow")), P(), P(), P()),
        out_specs=P(None, ("wide", "narrow")),
        check_vma=False,
    )
```

```python
import functools

import jax
import jax.numpy as jnp
from jax import lax
from jax.experimental import pallas as pl
from jax.experimental.pallas import tpu as pltpu
from jax.sharding import PartitionSpec as P

LANE_BITS = 7
LANES = 2**LANE_BITS
HALF = LANES // 2
CHUNKS = 2
MESH = pl.DeviceIdType.MESH
F32 = jnp.float32
BF16 = jnp.bfloat16


def log2(value):
    return value.bit_length() - 1


def partner(index, distance):
    result = index
    bit = 1
    while bit <= distance:
        if distance & bit:
            result = result + bit - 2 * bit * lax.rem(lax.div(index, bit), 2)
        bit *= 2
    return result


def one_hot(lane_values, rows):
    columns = lane_values.shape[1]
    row = lax.broadcasted_iota(jnp.int32, (rows, columns), 0)
    return jnp.where(row == lane_values, 1.0, 0.0).astype(BF16)


def split(values):
    high = values.astype(BF16)
    return high, (values - high.astype(F32)).astype(BF16)


def dot(a, b):
    return jnp.dot(a, b, preferred_element_type=F32)


class Layout:
    def __init__(self, free, wanted, row_bits):
        self.free = free
        self.row_bits = row_bits
        seen = jnp.int32(1) << free
        left = jnp.int32(row_bits - 2)
        packed = jnp.int32(0)
        for label in wanted:
            new = 1 - ((seen >> label) & 1)
            packed = packed + ((new * left) << (3 * label))
            left = left - new
            seen = seen | (jnp.int32(1) << label)
        for label in range(row_bits):
            new = 1 - ((seen >> label) & 1)
            packed = packed + ((new * left) << (3 * label))
            left = left - new
        self.packed = packed

    def inner(self, label):
        return (self.packed >> (3 * label)) & 7

    def shift(self, label):
        return jnp.where(label == self.free, self.row_bits - 1, self.inner(label))


def local_move(layout, free_next):
    differs = layout.free != free_next
    weights = [jnp.where(differs, 2, 1), jnp.where(differs, 1, 2)]

    def place(label):
        return jnp.where(label == layout.free, layout.row_bits - 2, layout.inner(label))

    return weights, place


def exchange_move(layout, slots, free_next):
    top = len(slots) + 2
    base = layout.row_bits - top
    slot_places = [layout.shift(slot) - base for slot in slots]
    count = jnp.int32(0)
    low = [jnp.int32(0), jnp.int32(0)]
    sent_places = []
    for index in range(top):
        is_slot = jnp.int32(0)
        value = jnp.int32(0)
        for number, slot_place in enumerate(slot_places):
            hit = (slot_place == index).astype(jnp.int32)
            is_slot = is_slot + hit
            value = value + hit * (2 + number)
        sent_places.append(jnp.where(is_slot == 1, value, count))
        for number in range(2):
            low[number] = low[number] + jnp.where(
                (is_slot == 0) & (count == number), 1 << index, 0
            )
        count = count + 1 - is_slot
    send_weights = low + [jnp.int32(1) << slot_place for slot_place in slot_places]

    def look_up(table, position):
        total = jnp.int32(0)
        for index, entry in enumerate(table):
            total = total + jnp.where(position == index, entry, 0)
        return total

    free_place = look_up(sent_places, layout.shift(free_next) - base)
    load_weights = [
        jnp.where(free_place <= index, 2 << index, 1 << index) for index in range(top - 1)
    ] + [jnp.int32(1) << free_place]
    final = [
        place - jnp.where(place > free_place, 1, 0) for place in sent_places
    ]

    def place(label):
        shift = layout.shift(label)
        return jnp.where(shift < base, shift, base + look_up(final, shift - base))

    return send_weights, load_weights, place


def block_number(index, weights):
    total = jnp.int32(0)
    for bit, weight in enumerate(weights):
        if (index >> bit) & 1:
            total = total + weight
    return total & (2 ** len(weights) - 1)


def load_blocks(ref, weights):
    count, rows, _ = ref.shape
    halves = []
    for half in range(2):
        parts = [
            ref[block_number(half * (count // 2) + index, weights)]
            for index in range(count // 2)
        ]
        halves.append(jnp.concatenate(parts, axis=0))
    return jnp.concatenate(halves, axis=1)


def store_blocks(ref, halves):
    count, rows, lanes = ref.shape
    for half in range(2):
        ref[pl.ds(half * (count // 2), count // 2)] = halves[half].reshape(
            count // 2, rows, lanes
        )


def kernel(
    narrow,
    wide,
    bits_hbm,
    plan_hbm,
    state_hbm,
    gates_hbm,
    out_ref,
    bits_ref,
    plan_ref,
    state_ref,
    gates_ref,
    high_ref,
    low_ref,
    local_ref,
    narrow_out,
    narrow_send,
    narrow_recv_0,
    narrow_recv_1,
    wide_out,
    wide_send,
    wide_recv_0,
    wide_recv_1,
    table_sem,
    state_sem,
    gate_sem,
    narrow_send_sem,
    narrow_recv_sem,
    wide_send_sem,
    wide_recv_sem,
):
    gate_count, _, dim, _ = gates_ref.shape
    third = gate_count // 3
    qubits = log2(dim)
    rows = state_ref.shape[0] // 2
    row_bits = log2(rows)
    narrow_bits = log2(narrow)
    wide_bits = log2(wide)
    me = {"narrow": lax.axis_index("narrow"), "wide": lax.axis_index("wide")}
    sizes = {"narrow": narrow, "wide": wide}
    narrow_recv = (narrow_recv_0, narrow_recv_1)
    wide_recv = (wide_recv_0, wide_recv_1)

    table_copies = [
        pltpu.make_async_copy(bits_hbm, bits_ref, table_sem.at[0]),
        pltpu.make_async_copy(plan_hbm, plan_ref, table_sem.at[1]),
    ]
    for copy in table_copies:
        copy.start()
    gate_copies = [
        pltpu.make_async_copy(gates_hbm.at[k], gates_ref.at[k], gate_sem.at[k])
        for k in range(gate_count)
    ]
    gate_copies[0].start()
    state_copy = pltpu.make_async_copy(state_hbm, state_ref, state_sem)
    state_copy.start()
    for k in range(1, third):
        gate_copies[k].start()

    barrier = pltpu.get_barrier_semaphore()
    for axis in ("narrow", "wide"):
        for step in reversed(range(1, sizes[axis])):
            peer = partner(me[axis], step)
            pl.semaphore_signal(
                barrier, inc=1, device_id={axis: peer}, device_id_type=MESH
            )

    for copy in table_copies:
        copy.wait()
    targets = [
        [bits_ref[k, j] - LANE_BITS for j in range(qubits)]
        for k in range(gate_count)
    ]
    free = [sum(range(row_bits)) - sum(targets[k]) for k in range(gate_count)]
    slots = [plan_ref[b] - LANE_BITS for b in range(narrow_bits + wide_bits)]
    crossing = {
        third - 1: slots[:narrow_bits],
        2 * third - 1: slots[narrow_bits:],
    }
    layouts, loads, sends, places = {}, {}, {}, {}

    def plan(k):
        layouts[k] = Layout(free[k], crossing.get(k, []) + [free[k + 1]], row_bits)
        if k in crossing:
            sends[k], loads[k], places[k + 1] = exchange_move(
                layouts[k], crossing[k], free[k + 1]
            )
        else:
            loads[k], places[k + 1] = local_move(layouts[k], free[k + 1])

    lane = lax.broadcasted_iota(jnp.int32, (1, dim), 1)

    def prepare(k):
        gate_copies[k].wait()
        pieces = [split(gates_ref[k, part]) for part in range(2)]
        if k > 0:
            column = sum(((lane >> places[k](targets[k][j])) & 1) << j for j in range(qubits))
            pick = one_hot(column, dim)
            pieces = [
                [dot(piece, pick).astype(BF16) for piece in both] for both in pieces
            ]
        if k < gate_count - 1:
            row = sum(
                ((lane >> j) & 1) << layouts[k].inner(targets[k][j]) for j in range(qubits)
            )
            pick_row = one_hot(row, dim)
            pieces = [
                [dot(pick_row, piece).astype(BF16) for piece in both] for both in pieces
            ]
        for part in range(2):
            high_ref[k, pl.ds(part * dim, dim)] = pieces[part][0]
            low_ref[k, pl.ds(part * dim, dim)] = pieces[part][1]

    first_half = lax.broadcasted_iota(jnp.int32, (dim, LANES), 1) < HALF

    def apply(k, halves):
        high, low = split(halves)
        total = dot(high_ref[k], high) + dot(high_ref[k], low) + dot(low_ref[k], high)
        results = []
        for half in range(2):
            by_real = total[:dim, half * LANES : (half + 1) * LANES]
            by_imag = pltpu.roll(
                total[dim:, half * LANES : (half + 1) * LANES], HALF, 1
            )
            results.append(by_real + jnp.where(first_half, -by_imag, by_imag))
        return results

    def copy_to(axis, chunk, send_ref, recv_ref, send_sems, recv_sems, peer):
        start = pl.ds(peer * 4, 4)
        return pltpu.make_async_remote_copy(
            src_ref=send_ref.at[chunk, start],
            dst_ref=recv_ref[chunk].at[pl.ds(me[axis] * 4, 4)],
            send_sem=send_sems.at[chunk, peer],
            recv_sem=recv_sems.at[chunk, me[axis]],
            device_id={axis: peer},
            device_id_type=MESH,
        )

    def copy_from(axis, chunk, send_ref, recv_ref, send_sems, recv_sems, peer):
        start = pl.ds(peer * 4, 4)
        return pltpu.make_async_remote_copy(
            src_ref=send_ref.at[chunk, start],
            dst_ref=recv_ref[chunk].at[start],
            send_sem=send_sems.at[chunk, peer],
            recv_sem=recv_sems.at[chunk, peer],
            device_id={axis: peer},
            device_id_type=MESH,
        )

    links = {
        "narrow": (narrow_send, narrow_recv, narrow_send_sem, narrow_recv_sem),
        "wide": (wide_send, wide_recv, wide_send_sem, wide_recv_sem),
    }

    def send(k, axis, chunk, out):
        send_ref, recv_ref = links[axis][:2]
        for index in range(out.shape[0]):
            send_ref[chunk, index] = out[block_number(index, sends[k])]
        for step in reversed(range(1, sizes[axis])):
            peer = partner(me[axis], step)
            copy_to(axis, chunk, *links[axis], peer).start()
        own = pl.ds(me[axis] * 4, 4)
        recv_ref[chunk][own] = send_ref[chunk, own]

    def receive(axis, chunk):
        for step in reversed(range(1, sizes[axis])):
            peer = partner(me[axis], step)
            copy_from(axis, chunk, *links[axis], peer).wait_recv()

    def section(first, chunk, halves, out):
        for k in range(first, first + third):
            results = apply(k, halves)
            if k < first + third - 1:
                held = local_ref.at[first // third, chunk]
                store_blocks(held, results)
                halves = load_blocks(held, loads[k])
        if out is not None:
            store_blocks(out, results)
        return results

    for k in range(third):
        plan(k)
    source = lax.broadcasted_iota(jnp.int32, (1, rows), 1)
    target = ((source >> free[0]) & 1) << (row_bits - 1)
    for j in range(qubits):
        target = target + (((source >> targets[0][j]) & 1) << j)
    order_in = one_hot(target, rows)
    prepare(0)
    state_copy.wait()
    real, imag = (state_ref[pl.ds(part, rows, stride=2), :] for part in range(2))
    whole_half = lax.broadcasted_iota(jnp.int32, (rows, LANES), 1) < HALF
    packed = [
        jnp.where(whole_half, real, pltpu.roll(imag, HALF, 1)),
        jnp.where(whole_half, pltpu.roll(real, HALF, 1), imag),
    ]
    for k in range(1, third):
        prepare(k)
    for k in range(third, gate_count):
        gate_copies[k].start()
    for chunk in range(CHUNKS):
        high, low = split(packed[chunk])
        ordered = dot(order_in, high) + dot(order_in, low)
        halves = jnp.concatenate([ordered[:dim], ordered[dim:]], axis=1)
        out = narrow_out.at[chunk]
        section(0, chunk, halves, out)
        if chunk == 0:
            pl.semaphore_wait(barrier, narrow + wide - 2)
        send(third - 1, "narrow", chunk, out)

    for k in range(third, gate_count - 1):
        plan(k)
    for k in range(third, gate_count):
        prepare(k)
    source = lax.broadcasted_iota(jnp.int32, (1, rows), 1)
    target = ((source >> (row_bits - 1)) & 1) << free[gate_count - 1]
    for j in range(qubits):
        target = target + (((source >> j) & 1) << targets[gate_count - 1][j])
    order_out = one_hot(target, rows)

    for chunk in range(CHUNKS):
        receive("narrow", chunk)
        halves = load_blocks(narrow_recv[chunk], loads[third - 1])
        out = wide_out.at[chunk]
        section(third, chunk, halves, out)
        send(2 * third - 1, "wide", chunk, out)

    final = []
    for chunk in range(CHUNKS):
        receive("wide", chunk)
        halves = load_blocks(wide_recv[chunk], loads[2 * third - 1])
        results = section(2 * third, chunk, halves, None)
        high, low = split(jnp.concatenate(results, axis=0))
        final.append(dot(order_out, high) + dot(order_out, low))
    out_ref[pl.ds(0, rows, stride=2), :] = jnp.where(
        whole_half, final[0], pltpu.roll(final[1], HALF, 1)
    )
    out_ref[pl.ds(1, rows, stride=2), :] = jnp.where(
        whole_half, pltpu.roll(final[0], HALF, 1), final[1]
    )

    for axis in ("narrow", "wide"):
        for chunk in range(CHUNKS):
            for step in reversed(range(1, sizes[axis])):
                peer = partner(me[axis], step)
                copy_to(axis, chunk, *links[axis], peer).wait_send()


def shards(state, gates, gate_bits, slot_plan):
    amount = state.shape[1]
    rows = amount // LANES
    narrow = lax.axis_size("narrow")
    wide = lax.axis_size("wide")
    gate_count, _, dim, _ = gates.shape

    def exchange_buffers(size):
        count = 4 * size
        block = (count, rows // count, LANES)
        return [pltpu.VMEM((CHUNKS, *block), F32)] * 2 + [pltpu.VMEM(block, F32)] * CHUNKS

    def sems(size):
        return [pltpu.SemaphoreType.DMA((CHUNKS, size))] * 2

    mixed = state.reshape(2, rows, LANES).transpose(1, 0, 2).reshape(2 * rows, LANES)
    result = pl.pallas_call(
        functools.partial(kernel, narrow, wide),
        out_shape=jax.ShapeDtypeStruct((2 * rows, LANES), F32),
        in_specs=[
            pl.BlockSpec(memory_space=pltpu.HBM),
            pl.BlockSpec(memory_space=pltpu.HBM),
            pl.BlockSpec(memory_space=pltpu.HBM),
            pl.BlockSpec(memory_space=pltpu.HBM),
        ],
        out_specs=pl.BlockSpec(memory_space=pltpu.VMEM),
        scratch_shapes=[
            pltpu.SMEM(gate_bits.shape, jnp.int32),
            pltpu.SMEM(slot_plan.shape, jnp.int32),
            pltpu.VMEM((2 * rows, LANES), F32),
            pltpu.VMEM(gates.shape, F32),
            pltpu.VMEM((gate_count, 2 * dim, dim), BF16),
            pltpu.VMEM((gate_count, 2 * dim, dim), BF16),
            pltpu.VMEM((3, CHUNKS, 4, rows // 4, LANES), F32),
            *exchange_buffers(narrow),
            *exchange_buffers(wide),
            pltpu.SemaphoreType.DMA((2,)),
            pltpu.SemaphoreType.DMA,
            pltpu.SemaphoreType.DMA((gate_count,)),
            *sems(narrow),
            *sems(wide),
        ],
        compiler_params=pltpu.CompilerParams(
            collective_id=0, has_side_effects=True, vmem_limit_bytes=32 * 2**20
        ),
        name="window",
    )(*(
        pltpu.with_memory_space_constraint(value, pltpu.HBM)
        for value in (gate_bits, slot_plan, mixed, gates)
    ))
    return result.reshape(rows, 2, LANES).transpose(1, 0, 2).reshape(2, amount)


def solution(mesh):
    return jax.shard_map(
        shards,
        mesh=mesh,
        in_specs=(P(None, ("wide", "narrow")), P(), P(), P()),
        out_specs=P(None, ("wide", "narrow")),
        check_vma=False,
    )
```

```python
import functools

import jax
import jax.numpy as jnp
from jax import lax
from jax.experimental import pallas as pl
from jax.experimental.pallas import tpu as pltpu
from jax.sharding import PartitionSpec as P

LANE_BITS = 7
LANES = 2**LANE_BITS
HALF = LANES // 2
CHUNKS = 2
MESH = pl.DeviceIdType.MESH
F32 = jnp.float32
BF16 = jnp.bfloat16


def log2(value):
    return value.bit_length() - 1


def partner(index, distance):
    result = index
    bit = 1
    while bit <= distance:
        if distance & bit:
            result = result + bit - 2 * bit * lax.rem(lax.div(index, bit), 2)
        bit *= 2
    return result


def one_hot(lane_values, rows):
    columns = lane_values.shape[1]
    row = lax.broadcasted_iota(jnp.int32, (rows, columns), 0)
    return jnp.where(row == lane_values, 1.0, 0.0).astype(BF16)


def split(values):
    high = values.astype(BF16)
    return high, (values - high.astype(F32)).astype(BF16)


def dot(a, b):
    return jnp.dot(a, b, preferred_element_type=F32)


def reorder(order, values):
    return dot(
        jnp.concatenate([order, order], axis=1), jnp.concatenate(split(values), axis=0)
    )


class Layout:
    def __init__(self, free, wanted, row_bits):
        self.free = free
        self.row_bits = row_bits
        seen = jnp.int32(1) << free
        left = jnp.int32(row_bits - 2)
        packed = jnp.int32(0)
        for label in wanted:
            new = 1 - ((seen >> label) & 1)
            packed = packed + ((new * left) << (3 * label))
            left = left - new
            seen = seen | (jnp.int32(1) << label)
        for label in range(row_bits):
            new = 1 - ((seen >> label) & 1)
            packed = packed + ((new * left) << (3 * label))
            left = left - new
        self.packed = packed

    def inner(self, label):
        return (self.packed >> (3 * label)) & 7

    def shift(self, label):
        return jnp.where(label == self.free, self.row_bits - 1, self.inner(label))


def local_move(layout, free_next):
    differs = layout.free != free_next
    weights = [jnp.where(differs, 2, 1), jnp.where(differs, 1, 2)]

    def place(label):
        return jnp.where(label == layout.free, layout.row_bits - 2, layout.inner(label))

    return weights, place


def exchange_move(layout, slots, free_next):
    top = len(slots) + 2
    base = layout.row_bits - top
    slot_places = [layout.shift(slot) - base for slot in slots]
    count = jnp.int32(0)
    low = [jnp.int32(0), jnp.int32(0)]
    sent_places = []
    for index in range(top):
        is_slot = jnp.int32(0)
        value = jnp.int32(0)
        for number, slot_place in enumerate(slot_places):
            hit = (slot_place == index).astype(jnp.int32)
            is_slot = is_slot + hit
            value = value + hit * (2 + number)
        sent_places.append(jnp.where(is_slot == 1, value, count))
        for number in range(2):
            low[number] = low[number] + jnp.where(
                (is_slot == 0) & (count == number), 1 << index, 0
            )
        count = count + 1 - is_slot
    send_weights = low + [jnp.int32(1) << slot_place for slot_place in slot_places]

    def look_up(table, position):
        total = jnp.int32(0)
        for index, entry in enumerate(table):
            total = total + jnp.where(position == index, entry, 0)
        return total

    free_place = look_up(sent_places, layout.shift(free_next) - base)
    load_weights = [
        jnp.where(free_place <= index, 2 << index, 1 << index) for index in range(top - 1)
    ] + [jnp.int32(1) << free_place]
    final = [
        place - jnp.where(place > free_place, 1, 0) for place in sent_places
    ]

    def place(label):
        shift = layout.shift(label)
        return jnp.where(shift < base, shift, base + look_up(final, shift - base))

    return send_weights, load_weights, place


def block_number(index, weights):
    total = jnp.int32(0)
    for bit, weight in enumerate(weights):
        if (index >> bit) & 1:
            total = total + weight
    return total & (2 ** len(weights) - 1)


def load_blocks(ref, weights):
    count, rows, _ = ref.shape
    halves = []
    for half in range(2):
        parts = [
            ref[block_number(half * (count // 2) + index, weights)]
            for index in range(count // 2)
        ]
        halves.append(jnp.concatenate(parts, axis=0))
    return jnp.concatenate(halves, axis=1)


def store_blocks(ref, halves):
    count, rows, lanes = ref.shape
    for half in range(2):
        ref[pl.ds(half * (count // 2), count // 2)] = halves[half].reshape(
            count // 2, rows, lanes
        )


def kernel(
    narrow,
    wide,
    bits_hbm,
    plan_hbm,
    state_hbm,
    gates_hbm,
    out_ref,
    bits_ref,
    plan_ref,
    state_ref,
    gates_ref,
    matrix_ref,
    local_ref,
    narrow_out,
    narrow_send,
    narrow_recv_0,
    narrow_recv_1,
    wide_out,
    wide_send,
    wide_recv_0,
    wide_recv_1,
    table_sem,
    state_sem,
    gate_sem,
    narrow_send_sem,
    narrow_recv_sem,
    wide_send_sem,
    wide_recv_sem,
):
    gate_count, _, dim, _ = gates_ref.shape
    third = gate_count // 3
    qubits = log2(dim)
    rows = state_ref.shape[0] // 2
    row_bits = log2(rows)
    narrow_bits = log2(narrow)
    wide_bits = log2(wide)
    me = {"narrow": lax.axis_index("narrow"), "wide": lax.axis_index("wide")}
    sizes = {"narrow": narrow, "wide": wide}
    narrow_recv = (narrow_recv_0, narrow_recv_1)
    wide_recv = (wide_recv_0, wide_recv_1)

    table_copies = [
        pltpu.make_async_copy(bits_hbm, bits_ref, table_sem.at[0]),
        pltpu.make_async_copy(plan_hbm, plan_ref, table_sem.at[1]),
    ]
    for copy in table_copies:
        copy.start()
    gate_copies = [
        pltpu.make_async_copy(gates_hbm.at[k], gates_ref.at[k], gate_sem.at[k])
        for k in range(gate_count)
    ]
    gate_copies[0].start()
    state_copy = pltpu.make_async_copy(state_hbm, state_ref, state_sem)
    state_copy.start()
    for k in range(1, third):
        gate_copies[k].start()

    barrier = pltpu.get_barrier_semaphore()
    for axis in ("narrow", "wide"):
        for step in reversed(range(1, sizes[axis])):
            peer = partner(me[axis], step)
            pl.semaphore_signal(
                barrier, inc=1, device_id={axis: peer}, device_id_type=MESH
            )

    for copy in table_copies:
        copy.wait()
    targets = [
        [bits_ref[k, j] - LANE_BITS for j in range(qubits)]
        for k in range(gate_count)
    ]
    free = [sum(range(row_bits)) - sum(targets[k]) for k in range(gate_count)]
    slots = [plan_ref[b] - LANE_BITS for b in range(narrow_bits + wide_bits)]
    crossing = {
        third - 1: slots[:narrow_bits],
        2 * third - 1: slots[narrow_bits:],
    }
    layouts, loads, sends, places = {}, {}, {}, {}

    def plan(k):
        layouts[k] = Layout(free[k], crossing.get(k, []) + [free[k + 1]], row_bits)
        if k in crossing:
            sends[k], loads[k], places[k + 1] = exchange_move(
                layouts[k], crossing[k], free[k + 1]
            )
        else:
            loads[k], places[k + 1] = local_move(layouts[k], free[k + 1])

    lane = lax.broadcasted_iota(jnp.int32, (1, dim), 1)

    def prepare(k):
        gate_copies[k].wait()
        both = split(gates_ref[k].reshape(2 * dim, dim))
        pieces = jnp.concatenate(both, axis=0)
        if k > 0:
            column = sum(((lane >> places[k](targets[k][j])) & 1) << j for j in range(qubits))
            pieces = dot(pieces, one_hot(column, dim)).astype(BF16)
        side = jnp.concatenate(
            [pieces[index * dim : (index + 1) * dim] for index in range(4)], axis=1
        )
        if k < gate_count - 1:
            row = sum(
                ((lane >> j) & 1) << layouts[k].inner(targets[k][j]) for j in range(qubits)
            )
            side = dot(one_hot(row, dim), side).astype(BF16)
        for part in range(2):
            high = side[:, part * dim : (part + 1) * dim]
            low = side[:, (2 + part) * dim : (3 + part) * dim]
            for number, piece in enumerate((high, high, low)):
                matrix_ref[k, pl.ds(part * dim, dim), pl.ds(number * dim, dim)] = piece

    first_half = lax.broadcasted_iota(jnp.int32, (dim, LANES), 1) < HALF

    def apply(k, halves):
        high, low = split(halves)
        total = dot(matrix_ref[k], jnp.concatenate([high, low, high], axis=0))
        results = []
        for half in range(2):
            by_real = total[:dim, half * LANES : (half + 1) * LANES]
            by_imag = pltpu.roll(
                total[dim:, half * LANES : (half + 1) * LANES], HALF, 1
            )
            results.append(by_real + jnp.where(first_half, -by_imag, by_imag))
        return results

    def copy_to(axis, chunk, send_ref, recv_ref, send_sems, recv_sems, peer):
        start = pl.ds(peer * 4, 4)
        return pltpu.make_async_remote_copy(
            src_ref=send_ref.at[chunk, start],
            dst_ref=recv_ref[chunk].at[pl.ds(me[axis] * 4, 4)],
            send_sem=send_sems.at[chunk, peer],
            recv_sem=recv_sems.at[chunk, me[axis]],
            device_id={axis: peer},
            device_id_type=MESH,
        )

    def copy_from(axis, chunk, send_ref, recv_ref, send_sems, recv_sems, peer):
        start = pl.ds(peer * 4, 4)
        return pltpu.make_async_remote_copy(
            src_ref=send_ref.at[chunk, start],
            dst_ref=recv_ref[chunk].at[start],
            send_sem=send_sems.at[chunk, peer],
            recv_sem=recv_sems.at[chunk, peer],
            device_id={axis: peer},
            device_id_type=MESH,
        )

    links = {
        "narrow": (narrow_send, narrow_recv, narrow_send_sem, narrow_recv_sem),
        "wide": (wide_send, wide_recv, wide_send_sem, wide_recv_sem),
    }

    def send(k, axis, chunk, out):
        send_ref, recv_ref = links[axis][:2]
        for index in range(out.shape[0]):
            send_ref[chunk, index] = out[block_number(index, sends[k])]
        for step in reversed(range(1, sizes[axis])):
            peer = partner(me[axis], step)
            copy_to(axis, chunk, *links[axis], peer).start()
        own = pl.ds(me[axis] * 4, 4)
        recv_ref[chunk][own] = send_ref[chunk, own]

    def receive(axis, chunk):
        for step in reversed(range(1, sizes[axis])):
            peer = partner(me[axis], step)
            copy_from(axis, chunk, *links[axis], peer).wait_recv()

    def section(first, chunk, halves, out):
        for k in range(first, first + third):
            results = apply(k, halves)
            if k < first + third - 1:
                held = local_ref.at[first // third, chunk]
                store_blocks(held, results)
                halves = load_blocks(held, loads[k])
        if out is not None:
            store_blocks(out, results)
        return results

    for k in range(third):
        plan(k)
    source = lax.broadcasted_iota(jnp.int32, (1, rows), 1)
    target = ((source >> free[0]) & 1) << (row_bits - 1)
    for j in range(qubits):
        target = target + (((source >> targets[0][j]) & 1) << j)
    order_in = one_hot(target, rows)
    prepare(0)
    state_copy.wait()
    real, imag = (state_ref[pl.ds(part, rows, stride=2), :] for part in range(2))
    whole_half = lax.broadcasted_iota(jnp.int32, (rows, LANES), 1) < HALF
    packed = [
        jnp.where(whole_half, real, pltpu.roll(imag, HALF, 1)),
        jnp.where(whole_half, pltpu.roll(real, HALF, 1), imag),
    ]
    for k in range(1, third):
        prepare(k)
    for k in range(third, gate_count):
        gate_copies[k].start()
    ordered_both = reorder(order_in, jnp.concatenate(packed, axis=1))
    for chunk in range(CHUNKS):
        ordered = ordered_both[:, chunk * LANES : (chunk + 1) * LANES]
        halves = jnp.concatenate([ordered[:dim], ordered[dim:]], axis=1)
        out = narrow_out.at[chunk]
        section(0, chunk, halves, out)
        if chunk == 0:
            pl.semaphore_wait(barrier, narrow + wide - 2)
        send(third - 1, "narrow", chunk, out)

    for k in range(third, gate_count - 1):
        plan(k)
    for k in range(third, gate_count):
        prepare(k)
    source = lax.broadcasted_iota(jnp.int32, (1, rows), 1)
    target = ((source >> (row_bits - 1)) & 1) << free[gate_count - 1]
    for j in range(qubits):
        target = target + (((source >> j) & 1) << targets[gate_count - 1][j])
    order_out = one_hot(target, rows)

    for chunk in range(CHUNKS):
        receive("narrow", chunk)
        halves = load_blocks(narrow_recv[chunk], loads[third - 1])
        out = wide_out.at[chunk]
        section(third, chunk, halves, out)
        send(2 * third - 1, "wide", chunk, out)

    final = []
    for chunk in range(CHUNKS):
        receive("wide", chunk)
        halves = load_blocks(wide_recv[chunk], loads[2 * third - 1])
        results = section(2 * third, chunk, halves, None)
        final.append(reorder(order_out, jnp.concatenate(results, axis=0)))
    out_ref[pl.ds(0, rows, stride=2), :] = jnp.where(
        whole_half, final[0], pltpu.roll(final[1], HALF, 1)
    )
    out_ref[pl.ds(1, rows, stride=2), :] = jnp.where(
        whole_half, pltpu.roll(final[0], HALF, 1), final[1]
    )

    for axis in ("narrow", "wide"):
        for chunk in range(CHUNKS):
            for step in reversed(range(1, sizes[axis])):
                peer = partner(me[axis], step)
                copy_to(axis, chunk, *links[axis], peer).wait_send()


def shards(state, gates, gate_bits, slot_plan):
    amount = state.shape[1]
    rows = amount // LANES
    narrow = lax.axis_size("narrow")
    wide = lax.axis_size("wide")
    gate_count, _, dim, _ = gates.shape

    def exchange_buffers(size):
        count = 4 * size
        block = (count, rows // count, LANES)
        return [pltpu.VMEM((CHUNKS, *block), F32)] * 2 + [pltpu.VMEM(block, F32)] * CHUNKS

    def sems(size):
        return [pltpu.SemaphoreType.DMA((CHUNKS, size))] * 2

    mixed = state.reshape(2, rows, LANES).transpose(1, 0, 2).reshape(2 * rows, LANES)
    result = pl.pallas_call(
        functools.partial(kernel, narrow, wide),
        out_shape=jax.ShapeDtypeStruct((2 * rows, LANES), F32),
        in_specs=[
            pl.BlockSpec(memory_space=pltpu.HBM),
            pl.BlockSpec(memory_space=pltpu.HBM),
            pl.BlockSpec(memory_space=pltpu.HBM),
            pl.BlockSpec(memory_space=pltpu.HBM),
        ],
        out_specs=pl.BlockSpec(memory_space=pltpu.VMEM),
        scratch_shapes=[
            pltpu.SMEM(gate_bits.shape, jnp.int32),
            pltpu.SMEM(slot_plan.shape, jnp.int32),
            pltpu.VMEM((2 * rows, LANES), F32),
            pltpu.VMEM(gates.shape, F32),
            pltpu.VMEM((gate_count, 2 * dim, 3 * dim), BF16),
            pltpu.VMEM((3, CHUNKS, 4, rows // 4, LANES), F32),
            *exchange_buffers(narrow),
            *exchange_buffers(wide),
            pltpu.SemaphoreType.DMA((2,)),
            pltpu.SemaphoreType.DMA,
            pltpu.SemaphoreType.DMA((gate_count,)),
            *sems(narrow),
            *sems(wide),
        ],
        compiler_params=pltpu.CompilerParams(
            collective_id=0, has_side_effects=True, vmem_limit_bytes=32 * 2**20
        ),
        name="window",
    )(*(
        pltpu.with_memory_space_constraint(value, pltpu.HBM)
        for value in (gate_bits, slot_plan, mixed, gates)
    ))
    return result.reshape(rows, 2, LANES).transpose(1, 0, 2).reshape(2, amount)


def solution(mesh):
    return jax.shard_map(
        shards,
        mesh=mesh,
        in_specs=(P(None, ("wide", "narrow")), P(), P(), P()),
        out_specs=P(None, ("wide", "narrow")),
        check_vma=False,
    )
```

```python
import functools

import jax
import jax.numpy as jnp
from jax import lax
from jax.experimental import pallas as pl
from jax.experimental.pallas import tpu as pltpu
from jax.sharding import PartitionSpec as P

LANE_BITS = 7
LANES = 2**LANE_BITS
HALF = LANES // 2
CHUNKS = 2
MESH = pl.DeviceIdType.MESH
F32 = jnp.float32
BF16 = jnp.bfloat16


def log2(value):
    return value.bit_length() - 1


def partner(index, distance):
    result = index
    bit = 1
    while bit <= distance:
        if distance & bit:
            result = result + bit - 2 * bit * lax.rem(lax.div(index, bit), 2)
        bit *= 2
    return result


def one_hot(lane_values, rows):
    columns = lane_values.shape[1]
    row = lax.broadcasted_iota(jnp.int32, (rows, columns), 0)
    return jnp.where(row == lane_values, 1.0, 0.0).astype(BF16)


def split(values):
    high = values.astype(BF16)
    return high, (values - high.astype(F32)).astype(BF16)


def dot(a, b):
    return jnp.dot(a, b, preferred_element_type=F32)


def reorder(order, values):
    return dot(
        jnp.concatenate([order, order], axis=1), jnp.concatenate(split(values), axis=0)
    )


class Layout:
    def __init__(self, free, wanted, row_bits):
        self.free = free
        self.row_bits = row_bits
        seen = jnp.int32(1) << free
        left = jnp.int32(row_bits - 2)
        packed = jnp.int32(0)
        for label in wanted:
            new = 1 - ((seen >> label) & 1)
            packed = packed + ((new * left) << (3 * label))
            left = left - new
            seen = seen | (jnp.int32(1) << label)
        for label in range(row_bits):
            new = 1 - ((seen >> label) & 1)
            packed = packed + ((new * left) << (3 * label))
            left = left - new
        self.packed = packed

    def inner(self, label):
        return (self.packed >> (3 * label)) & 7

    def shift(self, label):
        return jnp.where(label == self.free, self.row_bits - 1, self.inner(label))


def local_move(layout, free_next):
    differs = layout.free != free_next
    weights = [jnp.where(differs, 2, 1), jnp.where(differs, 1, 2)]

    def place(label):
        return jnp.where(label == layout.free, layout.row_bits - 2, layout.inner(label))

    return weights, place


def exchange_move(layout, slots, free_next):
    top = len(slots) + 2
    base = layout.row_bits - top
    slot_places = [layout.shift(slot) - base for slot in slots]
    count = jnp.int32(0)
    low = [jnp.int32(0), jnp.int32(0)]
    sent_places = []
    for index in range(top):
        is_slot = jnp.int32(0)
        value = jnp.int32(0)
        for number, slot_place in enumerate(slot_places):
            hit = (slot_place == index).astype(jnp.int32)
            is_slot = is_slot + hit
            value = value + hit * (2 + number)
        sent_places.append(jnp.where(is_slot == 1, value, count))
        for number in range(2):
            low[number] = low[number] + jnp.where(
                (is_slot == 0) & (count == number), 1 << index, 0
            )
        count = count + 1 - is_slot
    send_weights = low + [jnp.int32(1) << slot_place for slot_place in slot_places]

    def look_up(table, position):
        total = jnp.int32(0)
        for index, entry in enumerate(table):
            total = total + jnp.where(position == index, entry, 0)
        return total

    free_place = look_up(sent_places, layout.shift(free_next) - base)
    load_weights = [
        jnp.where(free_place <= index, 2 << index, 1 << index) for index in range(top - 1)
    ] + [jnp.int32(1) << free_place]
    final = [
        place - jnp.where(place > free_place, 1, 0) for place in sent_places
    ]

    def place(label):
        shift = layout.shift(label)
        return jnp.where(shift < base, shift, base + look_up(final, shift - base))

    return send_weights, load_weights, place


def block_number(index, weights):
    total = jnp.int32(0)
    for bit, weight in enumerate(weights):
        if (index >> bit) & 1:
            total = total + weight
    return total & (2 ** len(weights) - 1)


def load_blocks(ref, weights):
    count, rows, _ = ref.shape
    halves = []
    for half in range(2):
        parts = [
            ref[block_number(half * (count // 2) + index, weights)]
            for index in range(count // 2)
        ]
        halves.append(jnp.concatenate(parts, axis=0))
    return jnp.concatenate(halves, axis=1)


def store_blocks(ref, halves):
    count, rows, lanes = ref.shape
    for half in range(2):
        ref[pl.ds(half * (count // 2), count // 2)] = halves[half].reshape(
            count // 2, rows, lanes
        )


def kernel(
    narrow,
    wide,
    bits_hbm,
    plan_hbm,
    state_hbm,
    gates_hbm,
    out_ref,
    bits_ref,
    plan_ref,
    state_ref,
    gates_ref,
    matrix_ref,
    local_ref,
    narrow_out,
    narrow_send,
    narrow_recv_0,
    narrow_recv_1,
    wide_out,
    wide_send,
    wide_recv_0,
    wide_recv_1,
    table_sem,
    state_sem,
    gate_sem,
    narrow_send_sem,
    narrow_recv_sem,
    wide_send_sem,
    wide_recv_sem,
):
    gate_count, _, dim, _ = gates_ref.shape
    third = gate_count // 3
    qubits = log2(dim)
    rows = state_ref.shape[0] // 2
    row_bits = log2(rows)
    narrow_bits = log2(narrow)
    wide_bits = log2(wide)
    me = {"narrow": lax.axis_index("narrow"), "wide": lax.axis_index("wide")}
    sizes = {"narrow": narrow, "wide": wide}
    narrow_recv = (narrow_recv_0, narrow_recv_1)
    wide_recv = (wide_recv_0, wide_recv_1)

    table_copies = [
        pltpu.make_async_copy(bits_hbm, bits_ref, table_sem.at[0]),
        pltpu.make_async_copy(plan_hbm, plan_ref, table_sem.at[1]),
    ]
    for copy in table_copies:
        copy.start()
    gate_copies = [
        pltpu.make_async_copy(gates_hbm.at[k], gates_ref.at[k], gate_sem.at[k])
        for k in range(gate_count)
    ]
    gate_copies[0].start()
    state_copy = pltpu.make_async_copy(state_hbm, state_ref, state_sem)
    state_copy.start()
    for k in range(1, third):
        gate_copies[k].start()

    barrier = pltpu.get_barrier_semaphore()
    for axis in ("narrow", "wide"):
        for step in reversed(range(1, sizes[axis])):
            peer = partner(me[axis], step)
            pl.semaphore_signal(
                barrier, inc=1, device_id={axis: peer}, device_id_type=MESH
            )

    for copy in table_copies:
        copy.wait()
    targets = [
        [bits_ref[k, j] - LANE_BITS for j in range(qubits)]
        for k in range(gate_count)
    ]
    free = [sum(range(row_bits)) - sum(targets[k]) for k in range(gate_count)]
    slots = [plan_ref[b] - LANE_BITS for b in range(narrow_bits + wide_bits)]
    crossing = {
        third - 1: slots[:narrow_bits],
        2 * third - 1: slots[narrow_bits:],
    }
    layouts, loads, sends, places = {}, {}, {}, {}

    def plan(k):
        layouts[k] = Layout(free[k], crossing.get(k, []) + [free[k + 1]], row_bits)
        if k in crossing:
            sends[k], loads[k], places[k + 1] = exchange_move(
                layouts[k], crossing[k], free[k + 1]
            )
        else:
            loads[k], places[k + 1] = local_move(layouts[k], free[k + 1])

    lane = lax.broadcasted_iota(jnp.int32, (1, dim), 1)

    def prepare(k):
        gate_copies[k].wait()
        both = split(gates_ref[k].reshape(2 * dim, dim))
        pieces = jnp.concatenate(both, axis=0)
        if k > 0:
            column = sum(((lane >> places[k](targets[k][j])) & 1) << j for j in range(qubits))
            pieces = dot(pieces, one_hot(column, dim)).astype(BF16)
        side = jnp.concatenate(
            [pieces[index * dim : (index + 1) * dim] for index in range(4)], axis=1
        )
        if k < gate_count - 1:
            row = sum(
                ((lane >> j) & 1) << layouts[k].inner(targets[k][j]) for j in range(qubits)
            )
            side = dot(one_hot(row, dim), side).astype(BF16)
        for part in range(2):
            high = side[:, part * dim : (part + 1) * dim]
            low = side[:, (2 + part) * dim : (3 + part) * dim]
            for number, piece in enumerate((high, high, low)):
                matrix_ref[k, pl.ds(part * dim, dim), pl.ds(number * dim, dim)] = piece

    first_half = lax.broadcasted_iota(jnp.int32, (dim, LANES), 1) < HALF

    def apply(k, halves):
        high, low = split(halves)
        total = dot(matrix_ref[k], jnp.concatenate([high, low, high], axis=0))
        results = []
        for half in range(2):
            by_real = total[:dim, half * LANES : (half + 1) * LANES]
            by_imag = pltpu.roll(
                total[dim:, half * LANES : (half + 1) * LANES], HALF, 1
            )
            results.append(by_real + jnp.where(first_half, -by_imag, by_imag))
        return results

    def copy_to(axis, chunk, send_ref, recv_ref, send_sems, recv_sems, peer):
        start = pl.ds(peer * 4, 4)
        return pltpu.make_async_remote_copy(
            src_ref=send_ref.at[chunk, start],
            dst_ref=recv_ref[chunk].at[pl.ds(me[axis] * 4, 4)],
            send_sem=send_sems.at[chunk, peer],
            recv_sem=recv_sems.at[chunk, me[axis]],
            device_id={axis: peer},
            device_id_type=MESH,
        )

    def copy_from(axis, chunk, send_ref, recv_ref, send_sems, recv_sems, peer):
        start = pl.ds(peer * 4, 4)
        return pltpu.make_async_remote_copy(
            src_ref=send_ref.at[chunk, start],
            dst_ref=recv_ref[chunk].at[start],
            send_sem=send_sems.at[chunk, peer],
            recv_sem=recv_sems.at[chunk, peer],
            device_id={axis: peer},
            device_id_type=MESH,
        )

    links = {
        "narrow": (narrow_send, narrow_recv, narrow_send_sem, narrow_recv_sem),
        "wide": (wide_send, wide_recv, wide_send_sem, wide_recv_sem),
    }

    def pack(k, axis, chunk, out):
        send_ref, recv_ref = links[axis][:2]
        for index in range(out.shape[0]):
            send_ref[chunk, index] = out[block_number(index, sends[k])]
        own = pl.ds(me[axis] * 4, 4)
        recv_ref[chunk][own] = send_ref[chunk, own]

    def send(axis, chunk):
        for step in reversed(range(1, sizes[axis])):
            peer = partner(me[axis], step)
            if chunk > 0:
                copy_to(axis, chunk - 1, *links[axis], peer).wait_send()
            copy_to(axis, chunk, *links[axis], peer).start()

    def receive(axis, chunk):
        for step in reversed(range(1, sizes[axis])):
            peer = partner(me[axis], step)
            copy_from(axis, chunk, *links[axis], peer).wait_recv()

    def section(first, chunk, halves, out):
        for k in range(first, first + third):
            results = apply(k, halves)
            if k < first + third - 1:
                held = local_ref.at[first // third, chunk]
                store_blocks(held, results)
                halves = load_blocks(held, loads[k])
        if out is not None:
            store_blocks(out, results)
        return results

    for k in range(third):
        plan(k)
    source = lax.broadcasted_iota(jnp.int32, (1, rows), 1)
    target = ((source >> free[0]) & 1) << (row_bits - 1)
    for j in range(qubits):
        target = target + (((source >> targets[0][j]) & 1) << j)
    order_in = one_hot(target, rows)
    prepare(0)
    state_copy.wait()
    real, imag = (state_ref[pl.ds(part, rows, stride=2), :] for part in range(2))
    whole_half = lax.broadcasted_iota(jnp.int32, (rows, LANES), 1) < HALF
    packed = [
        jnp.where(whole_half, real, pltpu.roll(imag, HALF, 1)),
        jnp.where(whole_half, pltpu.roll(real, HALF, 1), imag),
    ]
    for k in range(1, third):
        prepare(k)
    for k in range(third, gate_count):
        gate_copies[k].start()
    ordered_both = reorder(order_in, jnp.concatenate(packed, axis=1))
    for chunk in range(CHUNKS):
        ordered = ordered_both[:, chunk * LANES : (chunk + 1) * LANES]
        halves = jnp.concatenate([ordered[:dim], ordered[dim:]], axis=1)
        out = narrow_out.at[chunk]
        section(0, chunk, halves, out)
        pack(third - 1, "narrow", chunk, out)
        if chunk == 0:
            pl.semaphore_wait(barrier, narrow + wide - 2)
        else:
            for k in range(third, 2 * third):
                plan(k)
                prepare(k)
        send("narrow", chunk)

    for k in range(2 * third, gate_count):
        if k < gate_count - 1:
            plan(k)
        prepare(k)
    source = lax.broadcasted_iota(jnp.int32, (1, rows), 1)
    target = ((source >> (row_bits - 1)) & 1) << free[gate_count - 1]
    for j in range(qubits):
        target = target + (((source >> j) & 1) << targets[gate_count - 1][j])
    order_out = one_hot(target, rows)

    for chunk in range(CHUNKS):
        receive("narrow", chunk)
        halves = load_blocks(narrow_recv[chunk], loads[third - 1])
        out = wide_out.at[chunk]
        section(third, chunk, halves, out)
        pack(2 * third - 1, "wide", chunk, out)
        send("wide", chunk)

    final = []
    for chunk in range(CHUNKS):
        receive("wide", chunk)
        halves = load_blocks(wide_recv[chunk], loads[2 * third - 1])
        results = section(2 * third, chunk, halves, None)
        final.append(reorder(order_out, jnp.concatenate(results, axis=0)))
    out_ref[pl.ds(0, rows, stride=2), :] = jnp.where(
        whole_half, final[0], pltpu.roll(final[1], HALF, 1)
    )
    out_ref[pl.ds(1, rows, stride=2), :] = jnp.where(
        whole_half, pltpu.roll(final[0], HALF, 1), final[1]
    )

    for axis in ("narrow", "wide"):
        for step in reversed(range(1, sizes[axis])):
            peer = partner(me[axis], step)
            copy_to(axis, CHUNKS - 1, *links[axis], peer).wait_send()


def shards(state, gates, gate_bits, slot_plan):
    amount = state.shape[1]
    rows = amount // LANES
    narrow = lax.axis_size("narrow")
    wide = lax.axis_size("wide")
    gate_count, _, dim, _ = gates.shape

    def exchange_buffers(size):
        count = 4 * size
        block = (count, rows // count, LANES)
        return [pltpu.VMEM((CHUNKS, *block), F32)] * 2 + [pltpu.VMEM(block, F32)] * CHUNKS

    def sems(size):
        return [pltpu.SemaphoreType.DMA((CHUNKS, size))] * 2

    mixed = state.reshape(2, rows, LANES).transpose(1, 0, 2).reshape(2 * rows, LANES)
    result = pl.pallas_call(
        functools.partial(kernel, narrow, wide),
        out_shape=jax.ShapeDtypeStruct((2 * rows, LANES), F32),
        in_specs=[
            pl.BlockSpec(memory_space=pltpu.HBM),
            pl.BlockSpec(memory_space=pltpu.HBM),
            pl.BlockSpec(memory_space=pltpu.HBM),
            pl.BlockSpec(memory_space=pltpu.HBM),
        ],
        out_specs=pl.BlockSpec(memory_space=pltpu.VMEM),
        scratch_shapes=[
            pltpu.SMEM(gate_bits.shape, jnp.int32),
            pltpu.SMEM(slot_plan.shape, jnp.int32),
            pltpu.VMEM((2 * rows, LANES), F32),
            pltpu.VMEM(gates.shape, F32),
            pltpu.VMEM((gate_count, 2 * dim, 3 * dim), BF16),
            pltpu.VMEM((3, CHUNKS, 4, rows // 4, LANES), F32),
            *exchange_buffers(narrow),
            *exchange_buffers(wide),
            pltpu.SemaphoreType.DMA((2,)),
            pltpu.SemaphoreType.DMA,
            pltpu.SemaphoreType.DMA((gate_count,)),
            *sems(narrow),
            *sems(wide),
        ],
        compiler_params=pltpu.CompilerParams(
            collective_id=0, has_side_effects=True, vmem_limit_bytes=32 * 2**20
        ),
        name="window",
    )(*(
        pltpu.with_memory_space_constraint(value, pltpu.HBM)
        for value in (gate_bits, slot_plan, mixed, gates)
    ))
    return result.reshape(rows, 2, LANES).transpose(1, 0, 2).reshape(2, amount)


def solution(mesh):
    return jax.shard_map(
        shards,
        mesh=mesh,
        in_specs=(P(None, ("wide", "narrow")), P(), P(), P()),
        out_specs=P(None, ("wide", "narrow")),
        check_vma=False,
    )
```

```python
import functools

import jax
import jax.numpy as jnp
from jax import lax
from jax.experimental import pallas as pl
from jax.experimental.pallas import tpu as pltpu
from jax.sharding import PartitionSpec as P

LANE_BITS = 7
LANES = 2**LANE_BITS
HALF = LANES // 2
CHUNKS = 2
MESH = pl.DeviceIdType.MESH
F32 = jnp.float32
BF16 = jnp.bfloat16


def log2(value):
    return value.bit_length() - 1


def partner(index, distance):
    result = index
    bit = 1
    while bit <= distance:
        if distance & bit:
            result = result + bit - 2 * bit * lax.rem(lax.div(index, bit), 2)
        bit *= 2
    return result


def line_order(index, size):
    mirrored = index >= size // 2
    place = jnp.where(mirrored, size - 1 - index, index)
    extra = size - 1 - 2 * place
    order = []
    for number in range(size - 1):
        later = jnp.maximum(number - extra, 0)
        distance = place - lax.div(later, 2)
        near = jnp.where(lax.rem(later, 2) == 0, place - distance, place + distance)
        peer = jnp.where(number < extra, size - 1 - number, near)
        order.append(jnp.where(mirrored, size - 1 - peer, peer))
    return order


def box_order(index, size):
    upper = log2(size) - 1
    odd = lax.rem(index, 2) == 1
    order = []
    for distance in reversed(range(1, size)):
        turned = distance & 1
        for bit in range(upper):
            turned |= ((distance >> (1 + bit)) & 1) << (upper - bit)
        order.append(jnp.where(odd, partner(index, turned), partner(index, distance)))
    return order


def one_hot(lane_values, rows):
    columns = lane_values.shape[1]
    row = lax.broadcasted_iota(jnp.int32, (rows, columns), 0)
    return jnp.where(row == lane_values, 1.0, 0.0).astype(BF16)


def split(values):
    high = values.astype(BF16)
    return high, (values - high.astype(F32)).astype(BF16)


def dot(a, b):
    return jnp.dot(a, b, preferred_element_type=F32)


def reorder(order, values):
    return dot(
        jnp.concatenate([order, order], axis=1), jnp.concatenate(split(values), axis=0)
    )


class Layout:
    def __init__(self, free, wanted, row_bits):
        self.free = free
        self.row_bits = row_bits
        seen = jnp.int32(1) << free
        left = jnp.int32(row_bits - 2)
        packed = jnp.int32(0)
        for label in wanted:
            new = 1 - ((seen >> label) & 1)
            packed = packed + ((new * left) << (3 * label))
            left = left - new
            seen = seen | (jnp.int32(1) << label)
        for label in range(row_bits):
            new = 1 - ((seen >> label) & 1)
            packed = packed + ((new * left) << (3 * label))
            left = left - new
        self.packed = packed

    def inner(self, label):
        return (self.packed >> (3 * label)) & 7

    def shift(self, label):
        return jnp.where(label == self.free, self.row_bits - 1, self.inner(label))


def local_move(layout, free_next):
    differs = layout.free != free_next
    weights = [jnp.where(differs, 2, 1), jnp.where(differs, 1, 2)]

    def place(label):
        return jnp.where(label == layout.free, layout.row_bits - 2, layout.inner(label))

    return weights, place


def exchange_move(layout, slots, free_next):
    top = len(slots) + 2
    base = layout.row_bits - top
    slot_places = [layout.shift(slot) - base for slot in slots]
    count = jnp.int32(0)
    low = [jnp.int32(0), jnp.int32(0)]
    sent_places = []
    for index in range(top):
        is_slot = jnp.int32(0)
        value = jnp.int32(0)
        for number, slot_place in enumerate(slot_places):
            hit = (slot_place == index).astype(jnp.int32)
            is_slot = is_slot + hit
            value = value + hit * (2 + number)
        sent_places.append(jnp.where(is_slot == 1, value, count))
        for number in range(2):
            low[number] = low[number] + jnp.where(
                (is_slot == 0) & (count == number), 1 << index, 0
            )
        count = count + 1 - is_slot
    send_weights = low + [jnp.int32(1) << slot_place for slot_place in slot_places]

    def look_up(table, position):
        total = jnp.int32(0)
        for index, entry in enumerate(table):
            total = total + jnp.where(position == index, entry, 0)
        return total

    free_place = look_up(sent_places, layout.shift(free_next) - base)
    load_weights = [
        jnp.where(free_place <= index, 2 << index, 1 << index) for index in range(top - 1)
    ] + [jnp.int32(1) << free_place]
    final = [
        place - jnp.where(place > free_place, 1, 0) for place in sent_places
    ]

    def place(label):
        shift = layout.shift(label)
        return jnp.where(shift < base, shift, base + look_up(final, shift - base))

    return send_weights, load_weights, place


def block_number(index, weights):
    total = jnp.int32(0)
    for bit, weight in enumerate(weights):
        if (index >> bit) & 1:
            total = total + weight
    return total & (2 ** len(weights) - 1)


def load_blocks(ref, weights):
    count, rows, _ = ref.shape
    halves = []
    for half in range(2):
        parts = [
            ref[block_number(half * (count // 2) + index, weights)]
            for index in range(count // 2)
        ]
        halves.append(jnp.concatenate(parts, axis=0))
    return jnp.concatenate(halves, axis=1)


def store_blocks(ref, halves):
    count, rows, lanes = ref.shape
    for half in range(2):
        ref[pl.ds(half * (count // 2), count // 2)] = halves[half].reshape(
            count // 2, rows, lanes
        )


def kernel(
    narrow,
    wide,
    bits_hbm,
    plan_hbm,
    state_hbm,
    gates_hbm,
    out_ref,
    bits_ref,
    plan_ref,
    state_ref,
    gates_ref,
    matrix_ref,
    local_ref,
    narrow_out,
    narrow_send,
    narrow_recv_0,
    narrow_recv_1,
    wide_out,
    wide_send,
    wide_recv_0,
    wide_recv_1,
    table_sem,
    state_sem,
    gate_sem,
    narrow_send_sem,
    narrow_recv_sem,
    wide_send_sem,
    wide_recv_sem,
):
    gate_count, _, dim, _ = gates_ref.shape
    third = gate_count // 3
    qubits = log2(dim)
    rows = state_ref.shape[0] // 2
    row_bits = log2(rows)
    narrow_bits = log2(narrow)
    wide_bits = log2(wide)
    me = {"narrow": lax.axis_index("narrow"), "wide": lax.axis_index("wide")}
    peers = {
        "narrow": line_order(me["narrow"], narrow),
        "wide": box_order(me["wide"], wide),
    }
    narrow_recv = (narrow_recv_0, narrow_recv_1)
    wide_recv = (wide_recv_0, wide_recv_1)

    table_copies = [
        pltpu.make_async_copy(bits_hbm, bits_ref, table_sem.at[0]),
        pltpu.make_async_copy(plan_hbm, plan_ref, table_sem.at[1]),
    ]
    for copy in table_copies:
        copy.start()
    gate_copies = [
        pltpu.make_async_copy(gates_hbm.at[k], gates_ref.at[k], gate_sem.at[k])
        for k in range(gate_count)
    ]
    gate_copies[0].start()
    state_copy = pltpu.make_async_copy(state_hbm, state_ref, state_sem)
    state_copy.start()
    for k in range(1, third):
        gate_copies[k].start()

    barrier = pltpu.get_barrier_semaphore()
    for axis in ("narrow", "wide"):
        for peer in peers[axis]:
            pl.semaphore_signal(
                barrier, inc=1, device_id={axis: peer}, device_id_type=MESH
            )

    for copy in table_copies:
        copy.wait()
    targets = [
        [bits_ref[k, j] - LANE_BITS for j in range(qubits)]
        for k in range(gate_count)
    ]
    free = [sum(range(row_bits)) - sum(targets[k]) for k in range(gate_count)]
    slots = [plan_ref[b] - LANE_BITS for b in range(narrow_bits + wide_bits)]
    crossing = {
        third - 1: slots[:narrow_bits],
        2 * third - 1: slots[narrow_bits:],
    }
    layouts, loads, sends, places = {}, {}, {}, {}

    def plan(k):
        layouts[k] = Layout(free[k], crossing.get(k, []) + [free[k + 1]], row_bits)
        if k in crossing:
            sends[k], loads[k], places[k + 1] = exchange_move(
                layouts[k], crossing[k], free[k + 1]
            )
        else:
            loads[k], places[k + 1] = local_move(layouts[k], free[k + 1])

    lane = lax.broadcasted_iota(jnp.int32, (1, dim), 1)

    def prepare(k):
        gate_copies[k].wait()
        both = split(gates_ref[k].reshape(2 * dim, dim))
        pieces = jnp.concatenate(both, axis=0)
        if k > 0:
            column = sum(((lane >> places[k](targets[k][j])) & 1) << j for j in range(qubits))
            pieces = dot(pieces, one_hot(column, dim)).astype(BF16)
        side = jnp.concatenate(
            [pieces[index * dim : (index + 1) * dim] for index in range(4)], axis=1
        )
        if k < gate_count - 1:
            row = sum(
                ((lane >> j) & 1) << layouts[k].inner(targets[k][j]) for j in range(qubits)
            )
            side = dot(one_hot(row, dim), side).astype(BF16)
        for part in range(2):
            high = side[:, part * dim : (part + 1) * dim]
            low = side[:, (2 + part) * dim : (3 + part) * dim]
            for number, piece in enumerate((high, high, low)):
                matrix_ref[k, pl.ds(part * dim, dim), pl.ds(number * dim, dim)] = piece

    first_half = lax.broadcasted_iota(jnp.int32, (dim, LANES), 1) < HALF

    def apply(k, halves):
        high, low = split(halves)
        total = dot(matrix_ref[k], jnp.concatenate([high, low, high], axis=0))
        results = []
        for half in range(2):
            by_real = total[:dim, half * LANES : (half + 1) * LANES]
            by_imag = pltpu.roll(
                total[dim:, half * LANES : (half + 1) * LANES], HALF, 1
            )
            results.append(by_real + jnp.where(first_half, -by_imag, by_imag))
        return results

    def copy_to(axis, chunk, send_ref, recv_ref, send_sems, recv_sems, peer):
        start = pl.ds(peer * 4, 4)
        return pltpu.make_async_remote_copy(
            src_ref=send_ref.at[chunk, start],
            dst_ref=recv_ref[chunk].at[pl.ds(me[axis] * 4, 4)],
            send_sem=send_sems.at[chunk, peer],
            recv_sem=recv_sems.at[chunk, me[axis]],
            device_id={axis: peer},
            device_id_type=MESH,
        )

    def copy_from(axis, chunk, send_ref, recv_ref, send_sems, recv_sems, peer):
        start = pl.ds(peer * 4, 4)
        return pltpu.make_async_remote_copy(
            src_ref=send_ref.at[chunk, start],
            dst_ref=recv_ref[chunk].at[start],
            send_sem=send_sems.at[chunk, peer],
            recv_sem=recv_sems.at[chunk, peer],
            device_id={axis: peer},
            device_id_type=MESH,
        )

    links = {
        "narrow": (narrow_send, narrow_recv, narrow_send_sem, narrow_recv_sem),
        "wide": (wide_send, wide_recv, wide_send_sem, wide_recv_sem),
    }

    def send(k, axis, chunk, out):
        send_ref, recv_ref = links[axis][:2]
        for index in range(out.shape[0]):
            send_ref[chunk, index] = out[block_number(index, sends[k])]
        for peer in peers[axis]:
            copy_to(axis, chunk, *links[axis], peer).start()
        own = pl.ds(me[axis] * 4, 4)
        recv_ref[chunk][own] = send_ref[chunk, own]

    def receive(axis, chunk):
        for peer in peers[axis]:
            copy_from(axis, chunk, *links[axis], peer).wait_recv()

    def section(first, chunk, halves, out):
        for k in range(first, first + third):
            results = apply(k, halves)
            if k < first + third - 1:
                held = local_ref.at[first // third, chunk]
                store_blocks(held, results)
                halves = load_blocks(held, loads[k])
        if out is not None:
            store_blocks(out, results)
        return results

    for k in range(third):
        plan(k)
    source = lax.broadcasted_iota(jnp.int32, (1, rows), 1)
    target = ((source >> free[0]) & 1) << (row_bits - 1)
    for j in range(qubits):
        target = target + (((source >> targets[0][j]) & 1) << j)
    order_in = one_hot(target, rows)
    prepare(0)
    state_copy.wait()
    real, imag = (state_ref[pl.ds(part, rows, stride=2), :] for part in range(2))
    whole_half = lax.broadcasted_iota(jnp.int32, (rows, LANES), 1) < HALF
    packed = [
        jnp.where(whole_half, real, pltpu.roll(imag, HALF, 1)),
        jnp.where(whole_half, pltpu.roll(real, HALF, 1), imag),
    ]
    for k in range(1, third):
        prepare(k)
    for k in range(third, gate_count):
        gate_copies[k].start()
    ordered_both = reorder(order_in, jnp.concatenate(packed, axis=1))
    for chunk in range(CHUNKS):
        ordered = ordered_both[:, chunk * LANES : (chunk + 1) * LANES]
        halves = jnp.concatenate([ordered[:dim], ordered[dim:]], axis=1)
        out = narrow_out.at[chunk]
        section(0, chunk, halves, out)
        if chunk == 0:
            pl.semaphore_wait(barrier, narrow + wide - 2)
        send(third - 1, "narrow", chunk, out)

    for k in range(third, gate_count - 1):
        plan(k)
    for k in range(third, gate_count):
        prepare(k)
    source = lax.broadcasted_iota(jnp.int32, (1, rows), 1)
    target = ((source >> (row_bits - 1)) & 1) << free[gate_count - 1]
    for j in range(qubits):
        target = target + (((source >> j) & 1) << targets[gate_count - 1][j])
    order_out = one_hot(target, rows)

    for chunk in range(CHUNKS):
        receive("narrow", chunk)
        halves = load_blocks(narrow_recv[chunk], loads[third - 1])
        out = wide_out.at[chunk]
        section(third, chunk, halves, out)
        send(2 * third - 1, "wide", chunk, out)

    final = []
    for chunk in range(CHUNKS):
        receive("wide", chunk)
        halves = load_blocks(wide_recv[chunk], loads[2 * third - 1])
        results = section(2 * third, chunk, halves, None)
        final.append(reorder(order_out, jnp.concatenate(results, axis=0)))
    out_ref[pl.ds(0, rows, stride=2), :] = jnp.where(
        whole_half, final[0], pltpu.roll(final[1], HALF, 1)
    )
    out_ref[pl.ds(1, rows, stride=2), :] = jnp.where(
        whole_half, pltpu.roll(final[0], HALF, 1), final[1]
    )

    for axis in ("narrow", "wide"):
        for chunk in range(CHUNKS):
            for peer in peers[axis]:
                copy_to(axis, chunk, *links[axis], peer).wait_send()


def shards(state, gates, gate_bits, slot_plan):
    amount = state.shape[1]
    rows = amount // LANES
    narrow = lax.axis_size("narrow")
    wide = lax.axis_size("wide")
    gate_count, _, dim, _ = gates.shape

    def exchange_buffers(size):
        count = 4 * size
        block = (count, rows // count, LANES)
        return [pltpu.VMEM((CHUNKS, *block), F32)] * 2 + [pltpu.VMEM(block, F32)] * CHUNKS

    def sems(size):
        return [pltpu.SemaphoreType.DMA((CHUNKS, size))] * 2

    mixed = state.reshape(2, rows, LANES).transpose(1, 0, 2).reshape(2 * rows, LANES)
    result = pl.pallas_call(
        functools.partial(kernel, narrow, wide),
        out_shape=jax.ShapeDtypeStruct((2 * rows, LANES), F32),
        in_specs=[
            pl.BlockSpec(memory_space=pltpu.HBM),
            pl.BlockSpec(memory_space=pltpu.HBM),
            pl.BlockSpec(memory_space=pltpu.HBM),
            pl.BlockSpec(memory_space=pltpu.HBM),
        ],
        out_specs=pl.BlockSpec(memory_space=pltpu.VMEM),
        scratch_shapes=[
            pltpu.SMEM(gate_bits.shape, jnp.int32),
            pltpu.SMEM(slot_plan.shape, jnp.int32),
            pltpu.VMEM((2 * rows, LANES), F32),
            pltpu.VMEM(gates.shape, F32),
            pltpu.VMEM((gate_count, 2 * dim, 3 * dim), BF16),
            pltpu.VMEM((3, CHUNKS, 4, rows // 4, LANES), F32),
            *exchange_buffers(narrow),
            *exchange_buffers(wide),
            pltpu.SemaphoreType.DMA((2,)),
            pltpu.SemaphoreType.DMA,
            pltpu.SemaphoreType.DMA((gate_count,)),
            *sems(narrow),
            *sems(wide),
        ],
        compiler_params=pltpu.CompilerParams(
            collective_id=0, has_side_effects=True, vmem_limit_bytes=32 * 2**20
        ),
        name="window",
    )(*(
        pltpu.with_memory_space_constraint(value, pltpu.HBM)
        for value in (gate_bits, slot_plan, mixed, gates)
    ))
    return result.reshape(rows, 2, LANES).transpose(1, 0, 2).reshape(2, amount)


def solution(mesh):
    return jax.shard_map(
        shards,
        mesh=mesh,
        in_specs=(P(None, ("wide", "narrow")), P(), P(), P()),
        out_specs=P(None, ("wide", "narrow")),
        check_vma=False,
    )
```

```python
import functools

import jax
import jax.numpy as jnp
from jax import lax
from jax.experimental import pallas as pl
from jax.experimental.pallas import tpu as pltpu
from jax.sharding import PartitionSpec as P

LANE_BITS = 7
LANES = 2**LANE_BITS
HALF = LANES // 2
CHUNKS = 2
MESH = pl.DeviceIdType.MESH
F32 = jnp.float32
BF16 = jnp.bfloat16


def log2(value):
    return value.bit_length() - 1


def partner(index, distance):
    result = index
    bit = 1
    while bit <= distance:
        if distance & bit:
            result = result + bit - 2 * bit * lax.rem(lax.div(index, bit), 2)
        bit *= 2
    return result


def line_order(index, size):
    mirrored = index >= size // 2
    place = jnp.where(mirrored, size - 1 - index, index)
    extra = size - 1 - 2 * place
    order = []
    for number in range(size - 1):
        later = jnp.maximum(number - extra, 0)
        distance = place - lax.div(later, 2)
        near = jnp.where(lax.rem(later, 2) == 0, place - distance, place + distance)
        peer = jnp.where(number < extra, size - 1 - number, near)
        order.append(jnp.where(mirrored, size - 1 - peer, peer))
    return order


def box_order(index, size):
    upper = log2(size) - 1
    odd = lax.rem(index, 2) == 1
    order = []
    for distance in reversed(range(1, size)):
        turned = distance & 1
        for bit in range(upper):
            turned |= ((distance >> (1 + bit)) & 1) << (upper - bit)
        order.append(jnp.where(odd, partner(index, turned), partner(index, distance)))
    return order


def one_hot(lane_values, rows):
    columns = lane_values.shape[1]
    row = lax.broadcasted_iota(jnp.int32, (rows, columns), 0)
    return jnp.where(row == lane_values, 1.0, 0.0).astype(BF16)


def split(values):
    high = values.astype(BF16)
    return high, (values - high.astype(F32)).astype(BF16)


def dot(a, b):
    return jnp.dot(a, b, preferred_element_type=F32)


def reorder(order, values):
    return dot(
        jnp.concatenate([order, order], axis=1), jnp.concatenate(split(values), axis=0)
    )


class Layout:
    def __init__(self, free, wanted, row_bits):
        self.free = free
        self.row_bits = row_bits
        seen = jnp.int32(1) << free
        left = jnp.int32(row_bits - 2)
        packed = jnp.int32(0)
        for label in wanted:
            new = 1 - ((seen >> label) & 1)
            packed = packed + ((new * left) << (3 * label))
            left = left - new
            seen = seen | (jnp.int32(1) << label)
        for label in range(row_bits):
            new = 1 - ((seen >> label) & 1)
            packed = packed + ((new * left) << (3 * label))
            left = left - new
        self.packed = packed

    def inner(self, label):
        return (self.packed >> (3 * label)) & 7

    def shift(self, label):
        return jnp.where(label == self.free, self.row_bits - 1, self.inner(label))


def local_move(layout, free_next):
    differs = layout.free != free_next
    weights = [jnp.where(differs, 2, 1), jnp.where(differs, 1, 2)]

    def place(label):
        return jnp.where(label == layout.free, layout.row_bits - 2, layout.inner(label))

    return weights, place


def exchange_move(layout, slots, free_next):
    top = len(slots) + 2
    base = layout.row_bits - top
    slot_places = [layout.shift(slot) - base for slot in slots]
    count = jnp.int32(0)
    low = [jnp.int32(0), jnp.int32(0)]
    sent_places = []
    for index in range(top):
        is_slot = jnp.int32(0)
        value = jnp.int32(0)
        for number, slot_place in enumerate(slot_places):
            hit = (slot_place == index).astype(jnp.int32)
            is_slot = is_slot + hit
            value = value + hit * (2 + number)
        sent_places.append(jnp.where(is_slot == 1, value, count))
        for number in range(2):
            low[number] = low[number] + jnp.where(
                (is_slot == 0) & (count == number), 1 << index, 0
            )
        count = count + 1 - is_slot
    send_weights = low + [jnp.int32(1) << slot_place for slot_place in slot_places]

    def look_up(table, position):
        total = jnp.int32(0)
        for index, entry in enumerate(table):
            total = total + jnp.where(position == index, entry, 0)
        return total

    free_place = look_up(sent_places, layout.shift(free_next) - base)
    load_weights = [
        jnp.where(free_place <= index, 2 << index, 1 << index) for index in range(top - 1)
    ] + [jnp.int32(1) << free_place]
    final = [
        place - jnp.where(place > free_place, 1, 0) for place in sent_places
    ]

    def place(label):
        shift = layout.shift(label)
        return jnp.where(shift < base, shift, base + look_up(final, shift - base))

    return send_weights, load_weights, place


def block_number(index, weights):
    total = jnp.int32(0)
    for bit, weight in enumerate(weights):
        if (index >> bit) & 1:
            total = total + weight
    return total & (2 ** len(weights) - 1)


def load_blocks(ref, weights):
    count, rows, _ = ref.shape
    halves = []
    for half in range(2):
        parts = [
            ref[block_number(half * (count // 2) + index, weights)]
            for index in range(count // 2)
        ]
        halves.append(jnp.concatenate(parts, axis=0))
    return jnp.concatenate(halves, axis=1)


def store_blocks(ref, halves):
    count, rows, lanes = ref.shape
    for half in range(2):
        ref[pl.ds(half * (count // 2), count // 2)] = halves[half].reshape(
            count // 2, rows, lanes
        )


def kernel(
    narrow,
    wide,
    bits_hbm,
    plan_hbm,
    state_hbm,
    gates_hbm,
    out_ref,
    bits_ref,
    plan_ref,
    state_ref,
    gates_ref,
    matrix_ref,
    local_ref,
    narrow_out,
    narrow_send,
    narrow_recv_0,
    narrow_recv_1,
    wide_out,
    wide_send,
    wide_recv_0,
    wide_recv_1,
    table_sem,
    state_sem,
    gate_sem,
    narrow_send_sem,
    narrow_recv_sem,
    wide_send_sem,
    wide_recv_sem,
):
    gate_count, _, dim, _ = gates_ref.shape
    third = gate_count // 3
    qubits = log2(dim)
    rows = state_ref.shape[0] // 2
    row_bits = log2(rows)
    narrow_bits = log2(narrow)
    wide_bits = log2(wide)
    me = {"narrow": lax.axis_index("narrow"), "wide": lax.axis_index("wide")}
    peers = {
        "narrow": line_order(me["narrow"], narrow),
        "wide": box_order(me["wide"], wide),
    }
    narrow_recv = (narrow_recv_0, narrow_recv_1)
    wide_recv = (wide_recv_0, wide_recv_1)

    table_copies = [
        pltpu.make_async_copy(bits_hbm, bits_ref, table_sem.at[0]),
        pltpu.make_async_copy(plan_hbm, plan_ref, table_sem.at[1]),
    ]
    for copy in table_copies:
        copy.start()
    gate_copies = [
        pltpu.make_async_copy(gates_hbm.at[k], gates_ref.at[k], gate_sem.at[k])
        for k in range(gate_count)
    ]
    gate_copies[0].start()
    state_copy = pltpu.make_async_copy(state_hbm, state_ref, state_sem)
    state_copy.start()
    for k in range(1, third):
        gate_copies[k].start()

    barrier = pltpu.get_barrier_semaphore()
    for axis in ("narrow", "wide"):
        for peer in peers[axis]:
            pl.semaphore_signal(
                barrier, inc=1, device_id={axis: peer}, device_id_type=MESH
            )

    for copy in table_copies:
        copy.wait()
    targets = [
        [bits_ref[k, j] - LANE_BITS for j in range(qubits)]
        for k in range(gate_count)
    ]
    free = [sum(range(row_bits)) - sum(targets[k]) for k in range(gate_count)]
    slots = [plan_ref[b] - LANE_BITS for b in range(narrow_bits + wide_bits)]
    crossing = {
        third - 1: slots[:narrow_bits],
        2 * third - 1: slots[narrow_bits:],
    }
    layouts, loads, sends, places = {}, {}, {}, {}

    def plan(k):
        layouts[k] = Layout(free[k], crossing.get(k, []) + [free[k + 1]], row_bits)
        if k in crossing:
            sends[k], loads[k], places[k + 1] = exchange_move(
                layouts[k], crossing[k], free[k + 1]
            )
        else:
            loads[k], places[k + 1] = local_move(layouts[k], free[k + 1])

    lane = lax.broadcasted_iota(jnp.int32, (1, dim), 1)

    def prepare(k):
        gate_copies[k].wait()
        both = split(gates_ref[k].reshape(2 * dim, dim))
        pieces = jnp.concatenate(both, axis=0)
        if k > 0:
            column = sum(((lane >> places[k](targets[k][j])) & 1) << j for j in range(qubits))
            pieces = dot(pieces, one_hot(column, dim)).astype(BF16)
        side = jnp.concatenate(
            [pieces[index * dim : (index + 1) * dim] for index in range(4)], axis=1
        )
        if k < gate_count - 1:
            row = sum(
                ((lane >> j) & 1) << layouts[k].inner(targets[k][j]) for j in range(qubits)
            )
            side = dot(one_hot(row, dim), side).astype(BF16)
        for part in range(2):
            high = side[:, part * dim : (part + 1) * dim]
            low = side[:, (2 + part) * dim : (3 + part) * dim]
            for number, piece in enumerate((high, high, low)):
                matrix_ref[k, pl.ds(part * dim, dim), pl.ds(number * dim, dim)] = piece

    first_half = lax.broadcasted_iota(jnp.int32, (dim, LANES), 1) < HALF

    def apply(k, halves):
        high, low = split(halves)
        total = dot(matrix_ref[k], jnp.concatenate([high, low, high], axis=0))
        results = []
        for half in range(2):
            by_real = total[:dim, half * LANES : (half + 1) * LANES]
            by_imag = pltpu.roll(
                total[dim:, half * LANES : (half + 1) * LANES], HALF, 1
            )
            results.append(by_real + jnp.where(first_half, -by_imag, by_imag))
        return results

    def copy_to(axis, chunk, send_ref, recv_ref, send_sems, recv_sems, peer):
        start = pl.ds(peer * 4, 4)
        return pltpu.make_async_remote_copy(
            src_ref=send_ref.at[chunk, start],
            dst_ref=recv_ref[chunk].at[pl.ds(me[axis] * 4, 4)],
            send_sem=send_sems.at[chunk, peer],
            recv_sem=recv_sems.at[chunk, me[axis]],
            device_id={axis: peer},
            device_id_type=MESH,
        )

    def copy_from(axis, chunk, send_ref, recv_ref, send_sems, recv_sems, peer):
        start = pl.ds(peer * 4, 4)
        return pltpu.make_async_remote_copy(
            src_ref=send_ref.at[chunk, start],
            dst_ref=recv_ref[chunk].at[start],
            send_sem=send_sems.at[chunk, peer],
            recv_sem=recv_sems.at[chunk, peer],
            device_id={axis: peer},
            device_id_type=MESH,
        )

    links = {
        "narrow": (narrow_send, narrow_recv, narrow_send_sem, narrow_recv_sem),
        "wide": (wide_send, wide_recv, wide_send_sem, wide_recv_sem),
    }

    def pack(k, axis, chunk, out):
        send_ref, recv_ref = links[axis][:2]
        for index in range(out.shape[0]):
            send_ref[chunk, index] = out[block_number(index, sends[k])]
        own = pl.ds(me[axis] * 4, 4)
        recv_ref[chunk][own] = send_ref[chunk, own]

    def send(axis, chunk, some):
        for peer in some:
            copy_to(axis, chunk, *links[axis], peer).start()

    def receive(axis, chunk):
        for peer in peers[axis]:
            copy_from(axis, chunk, *links[axis], peer).wait_recv()

    def section(first, chunk, halves, out):
        for k in range(first, first + third):
            results = apply(k, halves)
            if k < first + third - 1:
                held = local_ref.at[first // third, chunk]
                store_blocks(held, results)
                halves = load_blocks(held, loads[k])
        if out is not None:
            store_blocks(out, results)
        return results

    late = lax.rem(me["wide"], 2) == 1
    cut = (narrow - 1 + 2) // 3
    first_peers, other_peers = peers["narrow"][:cut], peers["narrow"][cut:]

    for k in range(third):
        plan(k)
    source = lax.broadcasted_iota(jnp.int32, (1, rows), 1)
    target = ((source >> free[0]) & 1) << (row_bits - 1)
    for j in range(qubits):
        target = target + (((source >> targets[0][j]) & 1) << j)
    order_in = one_hot(target, rows)
    prepare(0)
    state_copy.wait()
    real, imag = (state_ref[pl.ds(part, rows, stride=2), :] for part in range(2))
    whole_half = lax.broadcasted_iota(jnp.int32, (rows, LANES), 1) < HALF
    packed = [
        jnp.where(whole_half, real, pltpu.roll(imag, HALF, 1)),
        jnp.where(whole_half, pltpu.roll(real, HALF, 1), imag),
    ]
    for k in range(1, third):
        prepare(k)
    for k in range(third, gate_count):
        gate_copies[k].start()
    ordered_both = reorder(order_in, jnp.concatenate(packed, axis=1))
    for chunk in range(CHUNKS):
        ordered = ordered_both[:, chunk * LANES : (chunk + 1) * LANES]
        halves = jnp.concatenate([ordered[:dim], ordered[dim:]], axis=1)
        out = narrow_out.at[chunk]
        section(0, chunk, halves, out)
        if chunk == 0:
            pl.semaphore_wait(barrier, narrow + wide - 2)
        pack(third - 1, "narrow", chunk, out)
        if chunk == 0:
            send("narrow", chunk, peers["narrow"])
        else:
            send("narrow", chunk, first_peers)
            pl.when(jnp.logical_not(late))(
                functools.partial(send, "narrow", chunk, other_peers)
            )

    for k in range(third, gate_count - 1):
        plan(k)
    for k in range(third, gate_count):
        prepare(k)
    source = lax.broadcasted_iota(jnp.int32, (1, rows), 1)
    target = ((source >> (row_bits - 1)) & 1) << free[gate_count - 1]
    for j in range(qubits):
        target = target + (((source >> j) & 1) << targets[gate_count - 1][j])
    order_out = one_hot(target, rows)

    for chunk in range(CHUNKS):
        receive("narrow", chunk)
        halves = load_blocks(narrow_recv[chunk], loads[third - 1])
        out = wide_out.at[chunk]
        section(third, chunk, halves, out)
        pack(2 * third - 1, "wide", chunk, out)
        send("wide", chunk, peers["wide"])
        if chunk == 0:
            pl.when(late)(functools.partial(send, "narrow", CHUNKS - 1, other_peers))

    final = []
    for chunk in range(CHUNKS):
        receive("wide", chunk)
        halves = load_blocks(wide_recv[chunk], loads[2 * third - 1])
        results = section(2 * third, chunk, halves, None)
        final.append(reorder(order_out, jnp.concatenate(results, axis=0)))
    out_ref[pl.ds(0, rows, stride=2), :] = jnp.where(
        whole_half, final[0], pltpu.roll(final[1], HALF, 1)
    )
    out_ref[pl.ds(1, rows, stride=2), :] = jnp.where(
        whole_half, pltpu.roll(final[0], HALF, 1), final[1]
    )

    for axis in ("narrow", "wide"):
        for chunk in range(CHUNKS):
            for peer in peers[axis]:
                copy_to(axis, chunk, *links[axis], peer).wait_send()


def shards(state, gates, gate_bits, slot_plan):
    amount = state.shape[1]
    rows = amount // LANES
    narrow = lax.axis_size("narrow")
    wide = lax.axis_size("wide")
    gate_count, _, dim, _ = gates.shape

    def exchange_buffers(size):
        count = 4 * size
        block = (count, rows // count, LANES)
        return [pltpu.VMEM((CHUNKS, *block), F32)] * 2 + [pltpu.VMEM(block, F32)] * CHUNKS

    def sems(size):
        return [pltpu.SemaphoreType.DMA((CHUNKS, size))] * 2

    mixed = state.reshape(2, rows, LANES).transpose(1, 0, 2).reshape(2 * rows, LANES)
    result = pl.pallas_call(
        functools.partial(kernel, narrow, wide),
        out_shape=jax.ShapeDtypeStruct((2 * rows, LANES), F32),
        in_specs=[
            pl.BlockSpec(memory_space=pltpu.HBM),
            pl.BlockSpec(memory_space=pltpu.HBM),
            pl.BlockSpec(memory_space=pltpu.HBM),
            pl.BlockSpec(memory_space=pltpu.HBM),
        ],
        out_specs=pl.BlockSpec(memory_space=pltpu.VMEM),
        scratch_shapes=[
            pltpu.SMEM(gate_bits.shape, jnp.int32),
            pltpu.SMEM(slot_plan.shape, jnp.int32),
            pltpu.VMEM((2 * rows, LANES), F32),
            pltpu.VMEM(gates.shape, F32),
            pltpu.VMEM((gate_count, 2 * dim, 3 * dim), BF16),
            pltpu.VMEM((3, CHUNKS, 4, rows // 4, LANES), F32),
            *exchange_buffers(narrow),
            *exchange_buffers(wide),
            pltpu.SemaphoreType.DMA((2,)),
            pltpu.SemaphoreType.DMA,
            pltpu.SemaphoreType.DMA((gate_count,)),
            *sems(narrow),
            *sems(wide),
        ],
        compiler_params=pltpu.CompilerParams(
            collective_id=0, has_side_effects=True, vmem_limit_bytes=32 * 2**20
        ),
        name="window",
    )(*(
        pltpu.with_memory_space_constraint(value, pltpu.HBM)
        for value in (gate_bits, slot_plan, mixed, gates)
    ))
    return result.reshape(rows, 2, LANES).transpose(1, 0, 2).reshape(2, amount)


def solution(mesh):
    return jax.shard_map(
        shards,
        mesh=mesh,
        in_specs=(P(None, ("wide", "narrow")), P(), P(), P()),
        out_specs=P(None, ("wide", "narrow")),
        check_vma=False,
    )
```

```python
import functools

import jax
import jax.numpy as jnp
from jax import lax
from jax.experimental import pallas as pl
from jax.experimental.pallas import tpu as pltpu
from jax.sharding import PartitionSpec as P

LANE_BITS = 7
LANES = 2**LANE_BITS
HALF = LANES // 2
CHUNKS = 2
MESH = pl.DeviceIdType.MESH
F32 = jnp.float32
BF16 = jnp.bfloat16


def log2(value):
    return value.bit_length() - 1


def partner(index, distance):
    result = index
    bit = 1
    while bit <= distance:
        if distance & bit:
            result = result + bit - 2 * bit * lax.rem(lax.div(index, bit), 2)
        bit *= 2
    return result


def line_order(index, size, inner):
    mirrored = index >= size // 2
    place = jnp.where(mirrored, size - 1 - index, index)
    extra = size - 1 - 2 * place
    order = []
    for number in range(size - 1):
        later = jnp.maximum(number - extra, 0)
        distance = place - lax.div(later, 2)
        near = jnp.where(lax.rem(later, 2) == inner, place - distance, place + distance)
        peer = jnp.where(number < extra, size - 1 - number, near)
        order.append(jnp.where(mirrored, size - 1 - peer, peer))
    return order


def box_order(index, size):
    upper = log2(size) - 1
    odd = lax.rem(index, 2) == 1
    order = []
    for distance in reversed(range(1, size)):
        turned = distance & 1
        for bit in range(upper):
            turned |= ((distance >> (1 + bit)) & 1) << (upper - bit)
        order.append(jnp.where(odd, partner(index, turned), partner(index, distance)))
    return order


def one_hot(lane_values, rows):
    columns = lane_values.shape[1]
    row = lax.broadcasted_iota(jnp.int32, (rows, columns), 0)
    return jnp.where(row == lane_values, 1.0, 0.0).astype(BF16)


def split(values):
    high = values.astype(BF16)
    return high, (values - high.astype(F32)).astype(BF16)


def dot(a, b):
    return jnp.dot(a, b, preferred_element_type=F32)


def reorder(order, values):
    return dot(
        jnp.concatenate([order, order], axis=1), jnp.concatenate(split(values), axis=0)
    )


class Layout:
    def __init__(self, free, wanted, row_bits):
        self.free = free
        self.row_bits = row_bits
        seen = jnp.int32(1) << free
        left = jnp.int32(row_bits - 2)
        packed = jnp.int32(0)
        for label in wanted:
            new = 1 - ((seen >> label) & 1)
            packed = packed + ((new * left) << (3 * label))
            left = left - new
            seen = seen | (jnp.int32(1) << label)
        for label in range(row_bits):
            new = 1 - ((seen >> label) & 1)
            packed = packed + ((new * left) << (3 * label))
            left = left - new
        self.packed = packed

    def inner(self, label):
        return (self.packed >> (3 * label)) & 7

    def shift(self, label):
        return jnp.where(label == self.free, self.row_bits - 1, self.inner(label))


def local_move(layout, free_next):
    differs = layout.free != free_next
    weights = [jnp.where(differs, 2, 1), jnp.where(differs, 1, 2)]

    def place(label):
        return jnp.where(label == layout.free, layout.row_bits - 2, layout.inner(label))

    return weights, place


def exchange_move(layout, slots, free_next):
    top = len(slots) + 2
    base = layout.row_bits - top
    slot_places = [layout.shift(slot) - base for slot in slots]
    count = jnp.int32(0)
    low = [jnp.int32(0), jnp.int32(0)]
    sent_places = []
    for index in range(top):
        is_slot = jnp.int32(0)
        value = jnp.int32(0)
        for number, slot_place in enumerate(slot_places):
            hit = (slot_place == index).astype(jnp.int32)
            is_slot = is_slot + hit
            value = value + hit * (2 + number)
        sent_places.append(jnp.where(is_slot == 1, value, count))
        for number in range(2):
            low[number] = low[number] + jnp.where(
                (is_slot == 0) & (count == number), 1 << index, 0
            )
        count = count + 1 - is_slot
    send_weights = low + [jnp.int32(1) << slot_place for slot_place in slot_places]

    def look_up(table, position):
        total = jnp.int32(0)
        for index, entry in enumerate(table):
            total = total + jnp.where(position == index, entry, 0)
        return total

    free_place = look_up(sent_places, layout.shift(free_next) - base)
    load_weights = [
        jnp.where(free_place <= index, 2 << index, 1 << index) for index in range(top - 1)
    ] + [jnp.int32(1) << free_place]
    final = [
        place - jnp.where(place > free_place, 1, 0) for place in sent_places
    ]

    def place(label):
        shift = layout.shift(label)
        return jnp.where(shift < base, shift, base + look_up(final, shift - base))

    return send_weights, load_weights, place


def block_number(index, weights):
    total = jnp.int32(0)
    for bit, weight in enumerate(weights):
        if (index >> bit) & 1:
            total = total + weight
    return total & (2 ** len(weights) - 1)


def load_blocks(ref, weights):
    count, rows, _ = ref.shape
    halves = []
    for half in range(2):
        parts = [
            ref[block_number(half * (count // 2) + index, weights)]
            for index in range(count // 2)
        ]
        halves.append(jnp.concatenate(parts, axis=0))
    return jnp.concatenate(halves, axis=1)


def store_blocks(ref, halves):
    count, rows, lanes = ref.shape
    for half in range(2):
        ref[pl.ds(half * (count // 2), count // 2)] = halves[half].reshape(
            count // 2, rows, lanes
        )


def kernel(
    narrow,
    wide,
    bits_hbm,
    plan_hbm,
    state_hbm,
    gates_hbm,
    out_ref,
    bits_ref,
    plan_ref,
    state_ref,
    gates_ref,
    matrix_ref,
    local_ref,
    narrow_out,
    narrow_send,
    narrow_recv_0,
    narrow_recv_1,
    wide_out,
    wide_send,
    wide_recv_0,
    wide_recv_1,
    table_sem,
    state_sem,
    gate_sem,
    narrow_send_sem,
    narrow_recv_sem,
    wide_send_sem,
    wide_recv_sem,
):
    gate_count, _, dim, _ = gates_ref.shape
    third = gate_count // 3
    qubits = log2(dim)
    rows = state_ref.shape[0] // 2
    row_bits = log2(rows)
    narrow_bits = log2(narrow)
    wide_bits = log2(wide)
    me = {"narrow": lax.axis_index("narrow"), "wide": lax.axis_index("wide")}
    peers = {
        "narrow": line_order(me["narrow"], narrow, lax.rem(me["wide"], 2)),
        "wide": box_order(me["wide"], wide),
    }
    narrow_recv = (narrow_recv_0, narrow_recv_1)
    wide_recv = (wide_recv_0, wide_recv_1)

    table_copies = [
        pltpu.make_async_copy(bits_hbm, bits_ref, table_sem.at[0]),
        pltpu.make_async_copy(plan_hbm, plan_ref, table_sem.at[1]),
    ]
    for copy in table_copies:
        copy.start()
    gate_copies = [
        pltpu.make_async_copy(gates_hbm.at[k], gates_ref.at[k], gate_sem.at[k])
        for k in range(gate_count)
    ]
    gate_copies[0].start()
    state_copy = pltpu.make_async_copy(state_hbm, state_ref, state_sem)
    state_copy.start()
    for k in range(1, third):
        gate_copies[k].start()

    barrier = pltpu.get_barrier_semaphore()
    for axis in ("narrow", "wide"):
        for peer in peers[axis]:
            pl.semaphore_signal(
                barrier, inc=1, device_id={axis: peer}, device_id_type=MESH
            )

    for copy in table_copies:
        copy.wait()
    targets = [
        [bits_ref[k, j] - LANE_BITS for j in range(qubits)]
        for k in range(gate_count)
    ]
    free = [sum(range(row_bits)) - sum(targets[k]) for k in range(gate_count)]
    slots = [plan_ref[b] - LANE_BITS for b in range(narrow_bits + wide_bits)]
    crossing = {
        third - 1: slots[:narrow_bits],
        2 * third - 1: slots[narrow_bits:],
    }
    layouts, loads, sends, places = {}, {}, {}, {}

    def plan(k):
        layouts[k] = Layout(free[k], crossing.get(k, []) + [free[k + 1]], row_bits)
        if k in crossing:
            sends[k], loads[k], places[k + 1] = exchange_move(
                layouts[k], crossing[k], free[k + 1]
            )
        else:
            loads[k], places[k + 1] = local_move(layouts[k], free[k + 1])

    lane = lax.broadcasted_iota(jnp.int32, (1, dim), 1)

    def prepare(k):
        gate_copies[k].wait()
        both = split(gates_ref[k].reshape(2 * dim, dim))
        pieces = jnp.concatenate(both, axis=0)
        if k > 0:
            column = sum(((lane >> places[k](targets[k][j])) & 1) << j for j in range(qubits))
            pieces = dot(pieces, one_hot(column, dim)).astype(BF16)
        side = jnp.concatenate(
            [pieces[index * dim : (index + 1) * dim] for index in range(4)], axis=1
        )
        if k < gate_count - 1:
            row = sum(
                ((lane >> j) & 1) << layouts[k].inner(targets[k][j]) for j in range(qubits)
            )
            side = dot(one_hot(row, dim), side).astype(BF16)
        for part in range(2):
            high = side[:, part * dim : (part + 1) * dim]
            low = side[:, (2 + part) * dim : (3 + part) * dim]
            for number, piece in enumerate((high, high, low)):
                matrix_ref[k, pl.ds(part * dim, dim), pl.ds(number * dim, dim)] = piece

    first_half = lax.broadcasted_iota(jnp.int32, (dim, LANES), 1) < HALF

    def apply(k, halves):
        high, low = split(halves)
        total = dot(matrix_ref[k], jnp.concatenate([high, low, high], axis=0))
        results = []
        for half in range(2):
            by_real = total[:dim, half * LANES : (half + 1) * LANES]
            by_imag = pltpu.roll(
                total[dim:, half * LANES : (half + 1) * LANES], HALF, 1
            )
            results.append(by_real + jnp.where(first_half, -by_imag, by_imag))
        return results

    def copy_to(axis, chunk, send_ref, recv_ref, send_sems, recv_sems, peer):
        start = pl.ds(peer * 4, 4)
        return pltpu.make_async_remote_copy(
            src_ref=send_ref.at[chunk, start],
            dst_ref=recv_ref[chunk].at[pl.ds(me[axis] * 4, 4)],
            send_sem=send_sems.at[chunk, peer],
            recv_sem=recv_sems.at[chunk, me[axis]],
            device_id={axis: peer},
            device_id_type=MESH,
        )

    def copy_from(axis, chunk, send_ref, recv_ref, send_sems, recv_sems, peer):
        start = pl.ds(peer * 4, 4)
        return pltpu.make_async_remote_copy(
            src_ref=send_ref.at[chunk, start],
            dst_ref=recv_ref[chunk].at[start],
            send_sem=send_sems.at[chunk, peer],
            recv_sem=recv_sems.at[chunk, peer],
            device_id={axis: peer},
            device_id_type=MESH,
        )

    links = {
        "narrow": (narrow_send, narrow_recv, narrow_send_sem, narrow_recv_sem),
        "wide": (wide_send, wide_recv, wide_send_sem, wide_recv_sem),
    }

    def pack(k, axis, chunk, out):
        send_ref, recv_ref = links[axis][:2]
        for index in range(out.shape[0]):
            send_ref[chunk, index] = out[block_number(index, sends[k])]
        own = pl.ds(me[axis] * 4, 4)
        recv_ref[chunk][own] = send_ref[chunk, own]

    def send(axis, chunk, some):
        for peer in some:
            copy_to(axis, chunk, *links[axis], peer).start()

    def receive(axis, chunk):
        for peer in peers[axis]:
            copy_from(axis, chunk, *links[axis], peer).wait_recv()

    def section(first, chunk, halves, out):
        for k in range(first, first + third):
            results = apply(k, halves)
            if k < first + third - 1:
                held = local_ref.at[first // third, chunk]
                store_blocks(held, results)
                halves = load_blocks(held, loads[k])
        if out is not None:
            store_blocks(out, results)
        return results

    late = lax.rem(me["wide"], 2) == 1
    cut = (narrow - 1 + 2) // 3
    first_peers, other_peers = peers["narrow"][:cut], peers["narrow"][cut:]

    for k in range(third):
        plan(k)
    source = lax.broadcasted_iota(jnp.int32, (1, rows), 1)
    target = ((source >> free[0]) & 1) << (row_bits - 1)
    for j in range(qubits):
        target = target + (((source >> targets[0][j]) & 1) << j)
    order_in = one_hot(target, rows)
    prepare(0)
    state_copy.wait()
    real, imag = (state_ref[pl.ds(part, rows, stride=2), :] for part in range(2))
    whole_half = lax.broadcasted_iota(jnp.int32, (rows, LANES), 1) < HALF
    packed = [
        jnp.where(whole_half, real, pltpu.roll(imag, HALF, 1)),
        jnp.where(whole_half, pltpu.roll(real, HALF, 1), imag),
    ]
    for k in range(1, third):
        prepare(k)
    for k in range(third, gate_count):
        gate_copies[k].start()
    ordered_both = reorder(order_in, jnp.concatenate(packed, axis=1))
    for chunk in range(CHUNKS):
        ordered = ordered_both[:, chunk * LANES : (chunk + 1) * LANES]
        halves = jnp.concatenate([ordered[:dim], ordered[dim:]], axis=1)
        out = narrow_out.at[chunk]
        section(0, chunk, halves, out)
        if chunk == 0:
            pl.semaphore_wait(barrier, narrow + wide - 2)
        pack(third - 1, "narrow", chunk, out)
        if chunk == 0:
            send("narrow", chunk, peers["narrow"])
        else:
            send("narrow", chunk, first_peers)
            pl.when(jnp.logical_not(late))(
                functools.partial(send, "narrow", chunk, other_peers)
            )

    for k in range(third, gate_count - 1):
        plan(k)
    for k in range(third, gate_count):
        prepare(k)
    source = lax.broadcasted_iota(jnp.int32, (1, rows), 1)
    target = ((source >> (row_bits - 1)) & 1) << free[gate_count - 1]
    for j in range(qubits):
        target = target + (((source >> j) & 1) << targets[gate_count - 1][j])
    order_out = one_hot(target, rows)

    for chunk in range(CHUNKS):
        receive("narrow", chunk)
        halves = load_blocks(narrow_recv[chunk], loads[third - 1])
        out = wide_out.at[chunk]
        section(third, chunk, halves, out)
        pack(2 * third - 1, "wide", chunk, out)
        send("wide", chunk, peers["wide"])
        if chunk == 0:
            pl.when(late)(functools.partial(send, "narrow", CHUNKS - 1, other_peers))

    final = []
    for chunk in range(CHUNKS):
        receive("wide", chunk)
        halves = load_blocks(wide_recv[chunk], loads[2 * third - 1])
        results = section(2 * third, chunk, halves, None)
        final.append(reorder(order_out, jnp.concatenate(results, axis=0)))
    out_ref[pl.ds(0, rows, stride=2), :] = jnp.where(
        whole_half, final[0], pltpu.roll(final[1], HALF, 1)
    )
    out_ref[pl.ds(1, rows, stride=2), :] = jnp.where(
        whole_half, pltpu.roll(final[0], HALF, 1), final[1]
    )

    for axis in ("narrow", "wide"):
        for chunk in range(CHUNKS):
            for peer in peers[axis]:
                copy_to(axis, chunk, *links[axis], peer).wait_send()


def shards(state, gates, gate_bits, slot_plan):
    amount = state.shape[1]
    rows = amount // LANES
    narrow = lax.axis_size("narrow")
    wide = lax.axis_size("wide")
    gate_count, _, dim, _ = gates.shape

    def exchange_buffers(size):
        count = 4 * size
        block = (count, rows // count, LANES)
        return [pltpu.VMEM((CHUNKS, *block), F32)] * 2 + [pltpu.VMEM(block, F32)] * CHUNKS

    def sems(size):
        return [pltpu.SemaphoreType.DMA((CHUNKS, size))] * 2

    mixed = state.reshape(2, rows, LANES).transpose(1, 0, 2).reshape(2 * rows, LANES)
    result = pl.pallas_call(
        functools.partial(kernel, narrow, wide),
        out_shape=jax.ShapeDtypeStruct((2 * rows, LANES), F32),
        in_specs=[
            pl.BlockSpec(memory_space=pltpu.HBM),
            pl.BlockSpec(memory_space=pltpu.HBM),
            pl.BlockSpec(memory_space=pltpu.HBM),
            pl.BlockSpec(memory_space=pltpu.HBM),
        ],
        out_specs=pl.BlockSpec(memory_space=pltpu.VMEM),
        scratch_shapes=[
            pltpu.SMEM(gate_bits.shape, jnp.int32),
            pltpu.SMEM(slot_plan.shape, jnp.int32),
            pltpu.VMEM((2 * rows, LANES), F32),
            pltpu.VMEM(gates.shape, F32),
            pltpu.VMEM((gate_count, 2 * dim, 3 * dim), BF16),
            pltpu.VMEM((3, CHUNKS, 4, rows // 4, LANES), F32),
            *exchange_buffers(narrow),
            *exchange_buffers(wide),
            pltpu.SemaphoreType.DMA((2,)),
            pltpu.SemaphoreType.DMA,
            pltpu.SemaphoreType.DMA((gate_count,)),
            *sems(narrow),
            *sems(wide),
        ],
        compiler_params=pltpu.CompilerParams(
            collective_id=0, has_side_effects=True, vmem_limit_bytes=32 * 2**20
        ),
        name="window",
    )(*(
        pltpu.with_memory_space_constraint(value, pltpu.HBM)
        for value in (gate_bits, slot_plan, mixed, gates)
    ))
    return result.reshape(rows, 2, LANES).transpose(1, 0, 2).reshape(2, amount)


def solution(mesh):
    return jax.shard_map(
        shards,
        mesh=mesh,
        in_specs=(P(None, ("wide", "narrow")), P(), P(), P()),
        out_specs=P(None, ("wide", "narrow")),
        check_vma=False,
    )
```

```python
import functools

import jax
import jax.numpy as jnp
from jax import lax
from jax.experimental import pallas as pl
from jax.experimental.pallas import tpu as pltpu
from jax.sharding import PartitionSpec as P

LANE_BITS = 7
LANES = 2**LANE_BITS
HALF = LANES // 2
CHUNKS = 2
MESH = pl.DeviceIdType.MESH
F32 = jnp.float32
BF16 = jnp.bfloat16


def log2(value):
    return value.bit_length() - 1


def partner(index, distance):
    result = index
    bit = 1
    while bit <= distance:
        if distance & bit:
            result = result + bit - 2 * bit * lax.rem(lax.div(index, bit), 2)
        bit *= 2
    return result


def line_order(index, size, inner):
    mirrored = index >= size // 2
    place = jnp.where(mirrored, size - 1 - index, index)
    extra = size - 1 - 2 * place
    order = []
    for number in range(size - 1):
        later = jnp.maximum(number - extra, 0)
        distance = place - lax.div(later, 2)
        near = jnp.where(lax.rem(later, 2) == inner, place - distance, place + distance)
        peer = jnp.where(number < extra, size - 1 - number, near)
        order.append(jnp.where(mirrored, size - 1 - peer, peer))
    return order


def box_order(index, size):
    upper = log2(size) - 1
    odd = lax.rem(index, 2) == 1
    order = []
    for distance in reversed(range(1, size)):
        turned = distance & 1
        for bit in range(upper):
            turned |= ((distance >> (1 + bit)) & 1) << (upper - bit)
        order.append(jnp.where(odd, partner(index, turned), partner(index, distance)))
    return order


def one_hot(lane_values, rows):
    columns = lane_values.shape[1]
    row = lax.broadcasted_iota(jnp.int32, (rows, columns), 0)
    return jnp.where(row == lane_values, 1.0, 0.0).astype(BF16)


def split(values):
    high = values.astype(BF16)
    return high, (values - high.astype(F32)).astype(BF16)


def dot(a, b):
    return jnp.dot(a, b, preferred_element_type=F32)


def reorder(order, values):
    return dot(
        jnp.concatenate([order, order], axis=1), jnp.concatenate(split(values), axis=0)
    )


class Layout:
    def __init__(self, free, wanted, row_bits):
        self.free = free
        self.row_bits = row_bits
        seen = jnp.int32(1) << free
        left = jnp.int32(row_bits - 2)
        packed = jnp.int32(0)
        for label in wanted:
            new = 1 - ((seen >> label) & 1)
            packed = packed + ((new * left) << (3 * label))
            left = left - new
            seen = seen | (jnp.int32(1) << label)
        for label in range(row_bits):
            new = 1 - ((seen >> label) & 1)
            packed = packed + ((new * left) << (3 * label))
            left = left - new
        self.packed = packed

    def inner(self, label):
        return (self.packed >> (3 * label)) & 7

    def shift(self, label):
        return jnp.where(label == self.free, self.row_bits - 1, self.inner(label))


def local_move(layout, free_next):
    differs = layout.free != free_next
    weights = [jnp.where(differs, 2, 1), jnp.where(differs, 1, 2)]

    def place(label):
        return jnp.where(label == layout.free, layout.row_bits - 2, layout.inner(label))

    return weights, place


def exchange_move(layout, slots, free_next):
    top = len(slots) + 2
    base = layout.row_bits - top
    slot_places = [layout.shift(slot) - base for slot in slots]
    count = jnp.int32(0)
    low = [jnp.int32(0), jnp.int32(0)]
    sent_places = []
    for index in range(top):
        is_slot = jnp.int32(0)
        value = jnp.int32(0)
        for number, slot_place in enumerate(slot_places):
            hit = (slot_place == index).astype(jnp.int32)
            is_slot = is_slot + hit
            value = value + hit * (2 + number)
        sent_places.append(jnp.where(is_slot == 1, value, count))
        for number in range(2):
            low[number] = low[number] + jnp.where(
                (is_slot == 0) & (count == number), 1 << index, 0
            )
        count = count + 1 - is_slot
    send_weights = low + [jnp.int32(1) << slot_place for slot_place in slot_places]

    def look_up(table, position):
        total = jnp.int32(0)
        for index, entry in enumerate(table):
            total = total + jnp.where(position == index, entry, 0)
        return total

    free_place = look_up(sent_places, layout.shift(free_next) - base)
    load_weights = [
        jnp.where(free_place <= index, 2 << index, 1 << index) for index in range(top - 1)
    ] + [jnp.int32(1) << free_place]
    final = [
        place - jnp.where(place > free_place, 1, 0) for place in sent_places
    ]

    def place(label):
        shift = layout.shift(label)
        return jnp.where(shift < base, shift, base + look_up(final, shift - base))

    return send_weights, load_weights, place


def block_number(index, weights):
    total = jnp.int32(0)
    for bit, weight in enumerate(weights):
        if (index >> bit) & 1:
            total = total + weight
    return total & (2 ** len(weights) - 1)


def load_blocks(ref, weights):
    count, rows, _ = ref.shape
    halves = []
    for half in range(2):
        parts = [
            ref[block_number(half * (count // 2) + index, weights)]
            for index in range(count // 2)
        ]
        halves.append(jnp.concatenate(parts, axis=0))
    return jnp.concatenate(halves, axis=1)


def store_blocks(ref, halves):
    count, rows, lanes = ref.shape
    for half in range(2):
        ref[pl.ds(half * (count // 2), count // 2)] = halves[half].reshape(
            count // 2, rows, lanes
        )


def kernel(
    narrow,
    wide,
    bits_hbm,
    plan_hbm,
    state_hbm,
    gates_hbm,
    out_ref,
    bits_ref,
    plan_ref,
    state_ref,
    gates_ref,
    matrix_ref,
    local_ref,
    narrow_out,
    narrow_send,
    narrow_recv_0,
    narrow_recv_1,
    wide_out,
    wide_send,
    wide_recv_0,
    wide_recv_1,
    table_sem,
    state_sem,
    gate_sem,
    narrow_send_sem,
    narrow_recv_sem,
    wide_send_sem,
    wide_recv_sem,
):
    gate_count, _, dim, _ = gates_ref.shape
    third = gate_count // 3
    qubits = log2(dim)
    rows = state_ref.shape[0] // 2
    row_bits = log2(rows)
    narrow_bits = log2(narrow)
    wide_bits = log2(wide)
    me = {"narrow": lax.axis_index("narrow"), "wide": lax.axis_index("wide")}
    peers = {
        "narrow": line_order(me["narrow"], narrow, lax.rem(me["wide"], 2)),
        "wide": box_order(me["wide"], wide),
    }
    narrow_recv = (narrow_recv_0, narrow_recv_1)
    wide_recv = (wide_recv_0, wide_recv_1)

    table_copies = [
        pltpu.make_async_copy(bits_hbm, bits_ref, table_sem.at[0]),
        pltpu.make_async_copy(plan_hbm, plan_ref, table_sem.at[1]),
    ]
    for copy in table_copies:
        copy.start()
    gate_copies = [
        pltpu.make_async_copy(gates_hbm.at[k], gates_ref.at[k], gate_sem.at[k])
        for k in range(gate_count)
    ]
    gate_copies[0].start()
    state_copy = pltpu.make_async_copy(state_hbm, state_ref, state_sem)
    state_copy.start()
    for k in range(1, third):
        gate_copies[k].start()

    barrier = pltpu.get_barrier_semaphore()
    for axis in ("narrow", "wide"):
        for peer in peers[axis]:
            pl.semaphore_signal(
                barrier, inc=1, device_id={axis: peer}, device_id_type=MESH
            )

    for copy in table_copies:
        copy.wait()
    targets = [
        [bits_ref[k, j] - LANE_BITS for j in range(qubits)]
        for k in range(gate_count)
    ]
    free = [sum(range(row_bits)) - sum(targets[k]) for k in range(gate_count)]
    slots = [plan_ref[b] - LANE_BITS for b in range(narrow_bits + wide_bits)]
    crossing = {
        third - 1: slots[:narrow_bits],
        2 * third - 1: slots[narrow_bits:],
    }
    layouts, loads, sends, places = {}, {}, {}, {}

    def plan(k):
        layouts[k] = Layout(free[k], crossing.get(k, []) + [free[k + 1]], row_bits)
        if k in crossing:
            sends[k], loads[k], places[k + 1] = exchange_move(
                layouts[k], crossing[k], free[k + 1]
            )
        else:
            loads[k], places[k + 1] = local_move(layouts[k], free[k + 1])

    lane = lax.broadcasted_iota(jnp.int32, (1, dim), 1)

    def prepare(k):
        gate_copies[k].wait()
        both = split(gates_ref[k].reshape(2 * dim, dim))
        pieces = jnp.concatenate(both, axis=0)
        if k > 0:
            column = sum(((lane >> places[k](targets[k][j])) & 1) << j for j in range(qubits))
            pieces = dot(pieces, one_hot(column, dim)).astype(BF16)
        side = jnp.concatenate(
            [pieces[index * dim : (index + 1) * dim] for index in range(4)], axis=1
        )
        if k < gate_count - 1:
            row = sum(
                ((lane >> j) & 1) << layouts[k].inner(targets[k][j]) for j in range(qubits)
            )
            side = dot(one_hot(row, dim), side).astype(BF16)
        for part in range(2):
            high = side[:, part * dim : (part + 1) * dim]
            low = side[:, (2 + part) * dim : (3 + part) * dim]
            for number, piece in enumerate((high, high, low)):
                matrix_ref[k, pl.ds(part * dim, dim), pl.ds(number * dim, dim)] = piece

    first_half = lax.broadcasted_iota(jnp.int32, (dim, LANES), 1) < HALF

    def apply(k, halves):
        high, low = split(halves)
        total = dot(matrix_ref[k], jnp.concatenate([high, low, high], axis=0))
        results = []
        for half in range(2):
            by_real = total[:dim, half * LANES : (half + 1) * LANES]
            by_imag = pltpu.roll(
                total[dim:, half * LANES : (half + 1) * LANES], HALF, 1
            )
            results.append(by_real + jnp.where(first_half, -by_imag, by_imag))
        return results

    def copy_to(axis, chunk, send_ref, recv_ref, send_sems, recv_sems, peer):
        start = pl.ds(peer * 4, 4)
        return pltpu.make_async_remote_copy(
            src_ref=send_ref.at[chunk, start],
            dst_ref=recv_ref[chunk].at[pl.ds(me[axis] * 4, 4)],
            send_sem=send_sems.at[chunk, peer],
            recv_sem=recv_sems.at[chunk, me[axis]],
            device_id={axis: peer},
            device_id_type=MESH,
        )

    def copy_from(axis, chunk, send_ref, recv_ref, send_sems, recv_sems, peer):
        start = pl.ds(peer * 4, 4)
        return pltpu.make_async_remote_copy(
            src_ref=send_ref.at[chunk, start],
            dst_ref=recv_ref[chunk].at[start],
            send_sem=send_sems.at[chunk, peer],
            recv_sem=recv_sems.at[chunk, peer],
            device_id={axis: peer},
            device_id_type=MESH,
        )

    links = {
        "narrow": (narrow_send, narrow_recv, narrow_send_sem, narrow_recv_sem),
        "wide": (wide_send, wide_recv, wide_send_sem, wide_recv_sem),
    }

    def pack(k, axis, chunk, out):
        send_ref = links[axis][0]
        for index in range(out.shape[0]):
            send_ref[chunk, index] = out[block_number(index, sends[k])]

    def keep(axis, chunk):
        send_ref, recv_ref = links[axis][:2]
        own = pl.ds(me[axis] * 4, 4)
        recv_ref[chunk][own] = send_ref[chunk, own]

    def send(axis, chunk, some):
        for peer in some:
            copy_to(axis, chunk, *links[axis], peer).start()

    def receive(axis, chunk):
        keep(axis, chunk)
        for peer in peers[axis]:
            copy_from(axis, chunk, *links[axis], peer).wait_recv()

    def section(first, chunk, halves, out):
        for k in range(first, first + third):
            results = apply(k, halves)
            if k < first + third - 1:
                held = local_ref.at[first // third, chunk]
                store_blocks(held, results)
                halves = load_blocks(held, loads[k])
        if out is not None:
            store_blocks(out, results)
        return results

    late = lax.rem(me["wide"], 2) == 1
    cut = (narrow - 1 + 2) // 3
    first_peers, other_peers = peers["narrow"][:cut], peers["narrow"][cut:]

    for k in range(third):
        plan(k)
    source = lax.broadcasted_iota(jnp.int32, (1, rows), 1)
    target = ((source >> free[0]) & 1) << (row_bits - 1)
    for j in range(qubits):
        target = target + (((source >> targets[0][j]) & 1) << j)
    order_in = one_hot(target, rows)
    prepare(0)
    state_copy.wait()
    real, imag = (state_ref[pl.ds(part, rows, stride=2), :] for part in range(2))
    whole_half = lax.broadcasted_iota(jnp.int32, (rows, LANES), 1) < HALF
    packed = [
        jnp.where(whole_half, real, pltpu.roll(imag, HALF, 1)),
        jnp.where(whole_half, pltpu.roll(real, HALF, 1), imag),
    ]
    for k in range(1, third):
        prepare(k)
    for k in range(third, gate_count):
        gate_copies[k].start()
    ordered_both = reorder(order_in, jnp.concatenate(packed, axis=1))
    for chunk in range(CHUNKS):
        ordered = ordered_both[:, chunk * LANES : (chunk + 1) * LANES]
        halves = jnp.concatenate([ordered[:dim], ordered[dim:]], axis=1)
        out = narrow_out.at[chunk]
        section(0, chunk, halves, out)
        if chunk == 0:
            pl.semaphore_wait(barrier, narrow + wide - 2)
        pack(third - 1, "narrow", chunk, out)
        if chunk == 0:
            send("narrow", chunk, peers["narrow"])
        else:
            send("narrow", chunk, first_peers)
            pl.when(jnp.logical_not(late))(
                functools.partial(send, "narrow", chunk, other_peers)
            )

    for k in range(third, gate_count - 1):
        plan(k)
    for k in range(third, gate_count):
        prepare(k)
    source = lax.broadcasted_iota(jnp.int32, (1, rows), 1)
    target = ((source >> (row_bits - 1)) & 1) << free[gate_count - 1]
    for j in range(qubits):
        target = target + (((source >> j) & 1) << targets[gate_count - 1][j])
    order_out = one_hot(target, rows)

    for chunk in range(CHUNKS):
        receive("narrow", chunk)
        halves = load_blocks(narrow_recv[chunk], loads[third - 1])
        out = wide_out.at[chunk]
        section(third, chunk, halves, out)
        pack(2 * third - 1, "wide", chunk, out)
        send("wide", chunk, peers["wide"])
        if chunk == 0:
            pl.when(late)(functools.partial(send, "narrow", CHUNKS - 1, other_peers))

    final = []
    for chunk in range(CHUNKS):
        receive("wide", chunk)
        halves = load_blocks(wide_recv[chunk], loads[2 * third - 1])
        results = section(2 * third, chunk, halves, None)
        pieces = jnp.concatenate(split(jnp.concatenate(results, axis=0)), axis=1)
        ordered = dot(order_out, pieces)
        final.append(ordered[:, :LANES] + ordered[:, LANES:])
    out_ref[pl.ds(0, rows, stride=2), :] = jnp.where(
        whole_half, final[0], pltpu.roll(final[1], HALF, 1)
    )
    out_ref[pl.ds(1, rows, stride=2), :] = jnp.where(
        whole_half, pltpu.roll(final[0], HALF, 1), final[1]
    )

    for axis in ("narrow", "wide"):
        for chunk in range(CHUNKS):
            for peer in peers[axis]:
                copy_to(axis, chunk, *links[axis], peer).wait_send()


def shards(state, gates, gate_bits, slot_plan):
    amount = state.shape[1]
    rows = amount // LANES
    narrow = lax.axis_size("narrow")
    wide = lax.axis_size("wide")
    gate_count, _, dim, _ = gates.shape

    def exchange_buffers(size):
        count = 4 * size
        block = (count, rows // count, LANES)
        return [pltpu.VMEM((CHUNKS, *block), F32)] * 2 + [pltpu.VMEM(block, F32)] * CHUNKS

    def sems(size):
        return [pltpu.SemaphoreType.DMA((CHUNKS, size))] * 2

    mixed = state.reshape(2, rows, LANES).transpose(1, 0, 2).reshape(2 * rows, LANES)
    result = pl.pallas_call(
        functools.partial(kernel, narrow, wide),
        out_shape=jax.ShapeDtypeStruct((2 * rows, LANES), F32),
        in_specs=[
            pl.BlockSpec(memory_space=pltpu.HBM),
            pl.BlockSpec(memory_space=pltpu.HBM),
            pl.BlockSpec(memory_space=pltpu.HBM),
            pl.BlockSpec(memory_space=pltpu.HBM),
        ],
        out_specs=pl.BlockSpec(memory_space=pltpu.VMEM),
        scratch_shapes=[
            pltpu.SMEM(gate_bits.shape, jnp.int32),
            pltpu.SMEM(slot_plan.shape, jnp.int32),
            pltpu.VMEM((2 * rows, LANES), F32),
            pltpu.VMEM(gates.shape, F32),
            pltpu.VMEM((gate_count, 2 * dim, 3 * dim), BF16),
            pltpu.VMEM((3, CHUNKS, 4, rows // 4, LANES), F32),
            *exchange_buffers(narrow),
            *exchange_buffers(wide),
            pltpu.SemaphoreType.DMA((2,)),
            pltpu.SemaphoreType.DMA,
            pltpu.SemaphoreType.DMA((gate_count,)),
            *sems(narrow),
            *sems(wide),
        ],
        compiler_params=pltpu.CompilerParams(
            collective_id=0, has_side_effects=True, vmem_limit_bytes=32 * 2**20
        ),
        name="window",
    )(*(
        pltpu.with_memory_space_constraint(value, pltpu.HBM)
        for value in (gate_bits, slot_plan, mixed, gates)
    ))
    return result.reshape(rows, 2, LANES).transpose(1, 0, 2).reshape(2, amount)


def solution(mesh):
    return jax.shard_map(
        shards,
        mesh=mesh,
        in_specs=(P(None, ("wide", "narrow")), P(), P(), P()),
        out_specs=P(None, ("wide", "narrow")),
        check_vma=False,
    )
```

```python
import functools

import jax
import jax.numpy as jnp
from jax import lax
from jax.experimental import pallas as pl
from jax.experimental.pallas import tpu as pltpu
from jax.sharding import PartitionSpec as P

LANE_BITS = 7
LANES = 2**LANE_BITS
HALF = LANES // 2
CHUNKS = 2
MESH = pl.DeviceIdType.MESH
F32 = jnp.float32
BF16 = jnp.bfloat16


def log2(value):
    return value.bit_length() - 1


def partner(index, distance):
    result = index
    bit = 1
    while bit <= distance:
        if distance & bit:
            result = result + bit - 2 * bit * lax.rem(lax.div(index, bit), 2)
        bit *= 2
    return result


def line_order(index, size, inner):
    mirrored = index >= size // 2
    place = jnp.where(mirrored, size - 1 - index, index)
    extra = size - 1 - 2 * place
    order = []
    for number in range(size - 1):
        later = jnp.maximum(number - extra, 0)
        distance = place - lax.div(later, 2)
        near = jnp.where(lax.rem(later, 2) == inner, place - distance, place + distance)
        peer = jnp.where(number < extra, size - 1 - number, near)
        order.append(jnp.where(mirrored, size - 1 - peer, peer))
    return order


def box_order(index, size):
    upper = log2(size) - 1
    odd = lax.rem(index, 2) == 1
    order = []
    for distance in reversed(range(1, size)):
        turned = distance & 1
        for bit in range(upper):
            turned |= ((distance >> (1 + bit)) & 1) << (upper - bit)
        order.append(jnp.where(odd, partner(index, turned), partner(index, distance)))
    return order


def one_hot(lane_values, rows):
    columns = lane_values.shape[1]
    row = lax.broadcasted_iota(jnp.int32, (rows, columns), 0)
    return jnp.where(row == lane_values, 1.0, 0.0).astype(BF16)


def split(values):
    high = values.astype(BF16)
    return high, (values - high.astype(F32)).astype(BF16)


def dot(a, b):
    return jnp.dot(a, b, preferred_element_type=F32)


def reorder(order, values):
    return dot(
        jnp.concatenate([order, order], axis=1), jnp.concatenate(split(values), axis=0)
    )


class Layout:
    def __init__(self, free, wanted, row_bits):
        self.free = free
        self.row_bits = row_bits
        seen = jnp.int32(1) << free
        left = jnp.int32(row_bits - 2)
        packed = jnp.int32(0)
        for label in wanted:
            new = 1 - ((seen >> label) & 1)
            packed = packed + ((new * left) << (3 * label))
            left = left - new
            seen = seen | (jnp.int32(1) << label)
        for label in range(row_bits):
            new = 1 - ((seen >> label) & 1)
            packed = packed + ((new * left) << (3 * label))
            left = left - new
        self.packed = packed

    def inner(self, label):
        return (self.packed >> (3 * label)) & 7

    def shift(self, label):
        return jnp.where(label == self.free, self.row_bits - 1, self.inner(label))


def local_move(layout, free_next):
    differs = layout.free != free_next
    weights = [jnp.where(differs, 2, 1), jnp.where(differs, 1, 2)]

    def place(label):
        return jnp.where(label == layout.free, layout.row_bits - 2, layout.inner(label))

    return weights, place


def exchange_move(layout, slots, free_next):
    top = len(slots) + 2
    base = layout.row_bits - top
    slot_places = [layout.shift(slot) - base for slot in slots]
    count = jnp.int32(0)
    low = [jnp.int32(0), jnp.int32(0)]
    sent_places = []
    for index in range(top):
        is_slot = jnp.int32(0)
        value = jnp.int32(0)
        for number, slot_place in enumerate(slot_places):
            hit = (slot_place == index).astype(jnp.int32)
            is_slot = is_slot + hit
            value = value + hit * (2 + number)
        sent_places.append(jnp.where(is_slot == 1, value, count))
        for number in range(2):
            low[number] = low[number] + jnp.where(
                (is_slot == 0) & (count == number), 1 << index, 0
            )
        count = count + 1 - is_slot
    send_weights = low + [jnp.int32(1) << slot_place for slot_place in slot_places]

    def look_up(table, position):
        total = jnp.int32(0)
        for index, entry in enumerate(table):
            total = total + jnp.where(position == index, entry, 0)
        return total

    free_place = look_up(sent_places, layout.shift(free_next) - base)
    load_weights = [
        jnp.where(free_place <= index, 2 << index, 1 << index) for index in range(top - 1)
    ] + [jnp.int32(1) << free_place]
    final = [
        place - jnp.where(place > free_place, 1, 0) for place in sent_places
    ]

    def place(label):
        shift = layout.shift(label)
        return jnp.where(shift < base, shift, base + look_up(final, shift - base))

    return send_weights, load_weights, place


def block_number(index, weights):
    total = jnp.int32(0)
    for bit, weight in enumerate(weights):
        if (index >> bit) & 1:
            total = total + weight
    return total & (2 ** len(weights) - 1)


def load_blocks(ref, weights):
    count, rows, _ = ref.shape
    halves = []
    for half in range(2):
        parts = [
            ref[block_number(half * (count // 2) + index, weights)]
            for index in range(count // 2)
        ]
        halves.append(jnp.concatenate(parts, axis=0))
    return jnp.concatenate(halves, axis=1)


def store_blocks(ref, halves):
    count, rows, lanes = ref.shape
    for half in range(2):
        ref[pl.ds(half * (count // 2), count // 2)] = halves[half].reshape(
            count // 2, rows, lanes
        )


def kernel(
    narrow,
    wide,
    bits_hbm,
    plan_hbm,
    state_hbm,
    gates_hbm,
    out_ref,
    bits_ref,
    plan_ref,
    state_ref,
    gates_ref,
    matrix_ref,
    local_ref,
    narrow_out,
    narrow_send,
    narrow_recv_0,
    narrow_recv_1,
    wide_out,
    wide_send,
    wide_recv_0,
    wide_recv_1,
    table_sem,
    state_sem,
    gate_sem,
    narrow_send_sem,
    narrow_recv_sem,
    wide_send_sem,
    wide_recv_sem,
):
    gate_count, _, dim, _ = gates_ref.shape
    third = gate_count // 3
    qubits = log2(dim)
    rows = state_ref.shape[0] // 2
    row_bits = log2(rows)
    narrow_bits = log2(narrow)
    wide_bits = log2(wide)
    me = {"narrow": lax.axis_index("narrow"), "wide": lax.axis_index("wide")}
    peers = {
        "narrow": line_order(me["narrow"], narrow, lax.rem(me["wide"], 2)),
        "wide": box_order(me["wide"], wide),
    }
    narrow_recv = (narrow_recv_0, narrow_recv_1)
    wide_recv = (wide_recv_0, wide_recv_1)

    table_copies = [
        pltpu.make_async_copy(bits_hbm, bits_ref, table_sem.at[0]),
        pltpu.make_async_copy(plan_hbm, plan_ref, table_sem.at[1]),
    ]
    for copy in table_copies:
        copy.start()
    gate_copies = [
        pltpu.make_async_copy(gates_hbm.at[k], gates_ref.at[k], gate_sem.at[k])
        for k in range(gate_count)
    ]
    gate_copies[0].start()
    state_copy = pltpu.make_async_copy(state_hbm, state_ref, state_sem)
    state_copy.start()
    for k in range(1, third):
        gate_copies[k].start()

    barrier = pltpu.get_barrier_semaphore()
    for axis in ("narrow", "wide"):
        for peer in peers[axis]:
            pl.semaphore_signal(
                barrier, inc=1, device_id={axis: peer}, device_id_type=MESH
            )

    for copy in table_copies:
        copy.wait()
    targets = [
        [bits_ref[k, j] - LANE_BITS for j in range(qubits)]
        for k in range(gate_count)
    ]
    free = [sum(range(row_bits)) - sum(targets[k]) for k in range(gate_count)]
    slots = [plan_ref[b] - LANE_BITS for b in range(narrow_bits + wide_bits)]
    crossing = {
        third - 1: slots[:narrow_bits],
        2 * third - 1: slots[narrow_bits:],
    }
    layouts, loads, sends, places = {}, {}, {}, {}

    def plan(k):
        layouts[k] = Layout(free[k], crossing.get(k, []) + [free[k + 1]], row_bits)
        if k in crossing:
            sends[k], loads[k], places[k + 1] = exchange_move(
                layouts[k], crossing[k], free[k + 1]
            )
        else:
            loads[k], places[k + 1] = local_move(layouts[k], free[k + 1])

    lane = lax.broadcasted_iota(jnp.int32, (1, dim), 1)

    def prepare(k):
        gate_copies[k].wait()
        both = split(gates_ref[k].reshape(2 * dim, dim))
        pieces = jnp.concatenate(both, axis=0)
        if k > 0:
            column = sum(((lane >> places[k](targets[k][j])) & 1) << j for j in range(qubits))
            pieces = dot(pieces, one_hot(column, dim)).astype(BF16)
        side = jnp.concatenate(
            [pieces[index * dim : (index + 1) * dim] for index in range(4)], axis=1
        )
        if k < gate_count - 1:
            row = sum(
                ((lane >> j) & 1) << layouts[k].inner(targets[k][j]) for j in range(qubits)
            )
            side = dot(one_hot(row, dim), side).astype(BF16)
        for part in range(2):
            high = side[:, part * dim : (part + 1) * dim]
            low = side[:, (2 + part) * dim : (3 + part) * dim]
            for number, piece in enumerate((high, high, low)):
                matrix_ref[k, pl.ds(part * dim, dim), pl.ds(number * dim, dim)] = piece

    first_half = lax.broadcasted_iota(jnp.int32, (dim, LANES), 1) < HALF

    def apply(k, halves):
        high, low = split(halves)
        total = dot(matrix_ref[k], jnp.concatenate([high, low, high], axis=0))
        results = []
        for half in range(2):
            by_real = total[:dim, half * LANES : (half + 1) * LANES]
            by_imag = pltpu.roll(
                total[dim:, half * LANES : (half + 1) * LANES], HALF, 1
            )
            results.append(by_real + jnp.where(first_half, -by_imag, by_imag))
        return results

    def copy_to(axis, chunk, send_ref, recv_ref, send_sems, recv_sems, peer):
        start = pl.ds(peer * 4, 4)
        return pltpu.make_async_remote_copy(
            src_ref=send_ref.at[chunk, start],
            dst_ref=recv_ref[chunk].at[pl.ds(me[axis] * 4, 4)],
            send_sem=send_sems.at[chunk, peer],
            recv_sem=recv_sems.at[chunk, me[axis]],
            device_id={axis: peer},
            device_id_type=MESH,
        )

    def copy_from(axis, chunk, send_ref, recv_ref, send_sems, recv_sems, peer):
        start = pl.ds(peer * 4, 4)
        return pltpu.make_async_remote_copy(
            src_ref=send_ref.at[chunk, start],
            dst_ref=recv_ref[chunk].at[start],
            send_sem=send_sems.at[chunk, peer],
            recv_sem=recv_sems.at[chunk, peer],
            device_id={axis: peer},
            device_id_type=MESH,
        )

    links = {
        "narrow": (narrow_send, narrow_recv, narrow_send_sem, narrow_recv_sem),
        "wide": (wide_send, wide_recv, wide_send_sem, wide_recv_sem),
    }

    def pack(k, axis, chunk, out):
        send_ref = links[axis][0]
        for index in range(out.shape[0]):
            send_ref[chunk, index] = out[block_number(index, sends[k])]

    def keep(axis, chunk):
        send_ref, recv_ref = links[axis][:2]
        own = pl.ds(me[axis] * 4, 4)
        recv_ref[chunk][own] = send_ref[chunk, own]

    def send(axis, chunk, some):
        for peer in some:
            copy_to(axis, chunk, *links[axis], peer).start()

    def receive(axis, chunk):
        keep(axis, chunk)
        for peer in peers[axis]:
            copy_from(axis, chunk, *links[axis], peer).wait_recv()

    def section(first, chunk, halves, out):
        for k in range(first, first + third):
            results = apply(k, halves)
            if k < first + third - 1:
                held = local_ref.at[first // third, chunk]
                store_blocks(held, results)
                halves = load_blocks(held, loads[k])
        if out is not None:
            store_blocks(out, results)
        return results

    late = lax.rem(me["wide"], 2) == 1
    cut = (narrow - 1 + 2) // 3
    first_peers, other_peers = peers["narrow"][:cut], peers["narrow"][cut : 2 * cut]
    last_peers = peers["narrow"][2 * cut :]

    for k in range(third):
        plan(k)
    source = lax.broadcasted_iota(jnp.int32, (1, rows), 1)
    target = ((source >> free[0]) & 1) << (row_bits - 1)
    for j in range(qubits):
        target = target + (((source >> targets[0][j]) & 1) << j)
    order_in = one_hot(target, rows)
    prepare(0)
    state_copy.wait()
    real, imag = (state_ref[pl.ds(part, rows, stride=2), :] for part in range(2))
    whole_half = lax.broadcasted_iota(jnp.int32, (rows, LANES), 1) < HALF
    packed = [
        jnp.where(whole_half, real, pltpu.roll(imag, HALF, 1)),
        jnp.where(whole_half, pltpu.roll(real, HALF, 1), imag),
    ]
    for k in range(1, third):
        prepare(k)
    for k in range(third, gate_count):
        gate_copies[k].start()
    ordered_both = reorder(order_in, jnp.concatenate(packed, axis=1))
    for chunk in range(CHUNKS):
        ordered = ordered_both[:, chunk * LANES : (chunk + 1) * LANES]
        halves = jnp.concatenate([ordered[:dim], ordered[dim:]], axis=1)
        out = narrow_out.at[chunk]
        section(0, chunk, halves, out)
        if chunk == 0:
            pl.semaphore_wait(barrier, narrow + wide - 2)
        pack(third - 1, "narrow", chunk, out)
        if chunk == 0:
            send("narrow", chunk, peers["narrow"])
        else:
            send("narrow", chunk, first_peers)
            pl.when(jnp.logical_not(late))(
                functools.partial(send, "narrow", chunk, other_peers)
            )

    for k in range(third, gate_count - 1):
        plan(k)
    for k in range(third, gate_count):
        prepare(k)
    source = lax.broadcasted_iota(jnp.int32, (1, rows), 1)
    target = ((source >> (row_bits - 1)) & 1) << free[gate_count - 1]
    for j in range(qubits):
        target = target + (((source >> j) & 1) << targets[gate_count - 1][j])
    order_out = one_hot(target, rows)

    for chunk in range(CHUNKS):
        receive("narrow", chunk)
        halves = load_blocks(narrow_recv[chunk], loads[third - 1])
        out = wide_out.at[chunk]
        section(third, chunk, halves, out)
        pack(2 * third - 1, "wide", chunk, out)
        send("wide", chunk, peers["wide"])
        if chunk == 0:
            pl.when(late)(functools.partial(send, "narrow", CHUNKS - 1, other_peers))
            send("narrow", CHUNKS - 1, last_peers)

    final = []
    for chunk in range(CHUNKS):
        receive("wide", chunk)
        halves = load_blocks(wide_recv[chunk], loads[2 * third - 1])
        results = section(2 * third, chunk, halves, None)
        pieces = jnp.concatenate(split(jnp.concatenate(results, axis=0)), axis=1)
        ordered = dot(order_out, pieces)
        final.append(ordered[:, :LANES] + ordered[:, LANES:])
    out_ref[pl.ds(0, rows, stride=2), :] = jnp.where(
        whole_half, final[0], pltpu.roll(final[1], HALF, 1)
    )
    out_ref[pl.ds(1, rows, stride=2), :] = jnp.where(
        whole_half, pltpu.roll(final[0], HALF, 1), final[1]
    )

    for axis in ("narrow", "wide"):
        for chunk in range(CHUNKS):
            for peer in peers[axis]:
                copy_to(axis, chunk, *links[axis], peer).wait_send()


def shards(state, gates, gate_bits, slot_plan):
    amount = state.shape[1]
    rows = amount // LANES
    narrow = lax.axis_size("narrow")
    wide = lax.axis_size("wide")
    gate_count, _, dim, _ = gates.shape

    def exchange_buffers(size):
        count = 4 * size
        block = (count, rows // count, LANES)
        return [pltpu.VMEM((CHUNKS, *block), F32)] * 2 + [pltpu.VMEM(block, F32)] * CHUNKS

    def sems(size):
        return [pltpu.SemaphoreType.DMA((CHUNKS, size))] * 2

    mixed = state.reshape(2, rows, LANES).transpose(1, 0, 2).reshape(2 * rows, LANES)
    result = pl.pallas_call(
        functools.partial(kernel, narrow, wide),
        out_shape=jax.ShapeDtypeStruct((2 * rows, LANES), F32),
        in_specs=[
            pl.BlockSpec(memory_space=pltpu.HBM),
            pl.BlockSpec(memory_space=pltpu.HBM),
            pl.BlockSpec(memory_space=pltpu.HBM),
            pl.BlockSpec(memory_space=pltpu.HBM),
        ],
        out_specs=pl.BlockSpec(memory_space=pltpu.VMEM),
        scratch_shapes=[
            pltpu.SMEM(gate_bits.shape, jnp.int32),
            pltpu.SMEM(slot_plan.shape, jnp.int32),
            pltpu.VMEM((2 * rows, LANES), F32),
            pltpu.VMEM(gates.shape, F32),
            pltpu.VMEM((gate_count, 2 * dim, 3 * dim), BF16),
            pltpu.VMEM((3, CHUNKS, 4, rows // 4, LANES), F32),
            *exchange_buffers(narrow),
            *exchange_buffers(wide),
            pltpu.SemaphoreType.DMA((2,)),
            pltpu.SemaphoreType.DMA,
            pltpu.SemaphoreType.DMA((gate_count,)),
            *sems(narrow),
            *sems(wide),
        ],
        compiler_params=pltpu.CompilerParams(
            collective_id=0, has_side_effects=True, vmem_limit_bytes=32 * 2**20
        ),
        name="window",
    )(*(
        pltpu.with_memory_space_constraint(value, pltpu.HBM)
        for value in (gate_bits, slot_plan, mixed, gates)
    ))
    return result.reshape(rows, 2, LANES).transpose(1, 0, 2).reshape(2, amount)


def solution(mesh):
    return jax.shard_map(
        shards,
        mesh=mesh,
        in_specs=(P(None, ("wide", "narrow")), P(), P(), P()),
        out_specs=P(None, ("wide", "narrow")),
        check_vma=False,
    )
```
